32 devices in a mesh: brick: 4 (over y, x), gz: 8 (over z, core).
Axes of the slice: x: 2, y: 2, z: 4, core: 2. Of those that a mesh axis runs over, the one named last changes fastest.
Arguments:
- grad_field: float32 [5, 32, 512, 512], P(None, 'brick', 'gz'), may hold values from -3 to 3
- alpha_coef: float32 [5, 32], P(None, 'brick'), may hold values from 0.3 to 0.4
- metric_inner: float32 [32, 512], P('brick', 'gz'), may hold values from 0.5 to 2
- metric_outer: float32 [32, 512], P('brick', 'gz'), may hold values from 0.5 to 2
Outputs:
- adjoint_field: float32 [5, 32, 512, 512], P(None, 'brick', 'gz')
The draws below stay inside these ranges and needn't reach their ends.
All inputs are finite; a program needn't handle non-finite values.
Results may differ from the reference program's by a relative error of at most 0.00012.
Values sent between devices are 32-bit elements; how exact they have to be, the bound alone decides.
A program may use at most 64 MiB of HBM per device.

```python
import math
import jax
import jax.numpy as jnp

F = 5
NY = 512
NX = 32
NZ = 512


def steps_of(rng, shape, split, smallest, high):
    gain, own = 1.0, jax.random.fold_in(rng, 6)
    for position, shards_of in split:
        draws = jnp.exp(jax.random.uniform(jax.random.fold_in(own, position), (shards_of,), jnp.float32, smallest / len(split), high / len(split)))
        gain = gain * jnp.repeat(draws, shape[position] // shards_of).reshape([-1 if axis == position else 1 for axis in range(len(shape))])
    return gain


def normal_values(own_key, extent, scale, limit, cuts=(), kind=jnp.bfloat16):
    loudness = steps_of(own_key, extent, cuts, -0.22, 0.18) if cuts else 1.0
    values = jax.random.normal(own_key, extent, jnp.float32) * scale * loudness
    return jnp.minimum(jnp.maximum(values, -limit), limit).astype(kind)


def setup_inputs(seed: int = 0) -> dict:
    seeds = jax.random.split(jax.random.key(seed), 5)
    return {
        "grad_field": normal_values(seeds[0], (F, NX, NZ, NY), 0.5, 3.0, ((1, 4), (2, 8)), jnp.float32),
        "alpha_coef": jnp.clip(0.3 + 0.099999994 * jax.random.uniform(seeds[1], (F, NX), jnp.float32) ** steps_of(seeds[1], (F, NX), ((1, 4),), -0.2, 0.2), 0.3, 0.4),
        "metric_inner": jnp.clip(jnp.exp(math.log(2.0) - 1.3862944 * jax.random.uniform(seeds[2], (NX, NZ), jnp.float32) ** steps_of(seeds[2], (NX, NZ), ((0, 4), (1, 8)), -0.2, 0.2)), 0.5, 2.0),
        "metric_outer": jnp.clip(jnp.exp(math.log(2.0) - 1.3862944 * jax.random.uniform(seeds[3], (NX, NZ), jnp.float32) ** steps_of(seeds[3], (NX, NZ), ((0, 4), (1, 8)), -0.2, 0.2)), 0.5, 2.0),
    }


def solve_cyclic(values, alpha_coef):
    spectrum = jnp.fft.rfft(values, axis=2)
    wave = jnp.arange(NZ // 2 + 1).astype(jnp.float32)
    symbol = 1.0 + 2.0 * alpha_coef[:, :, None, None] * jnp.cos(2.0 * jnp.pi * wave / NZ)[None, None, :, None]
    return jnp.fft.irfft(spectrum / symbol, n=NZ, axis=2).astype(values.dtype)


def stencil_apply(values, alpha_coef):
    near_coef = (2.0 * (alpha_coef + 2.0) / 3.0)[:, :, None, None]
    far_coef = ((4.0 * alpha_coef - 1.0) / 3.0)[:, :, None, None]
    up_one = jnp.roll(values, -1, axis=2)
    down_one = jnp.roll(values, 1, axis=2)
    up_two = jnp.roll(values, -2, axis=2)
    down_two = jnp.roll(values, 2, axis=2)
    return -(near_coef * (up_one - down_one) * 0.5 + far_coef * (up_two - down_two) * 0.25)


def adjoint_pass(values, alpha_coef):
    return stencil_apply(solve_cyclic(values, alpha_coef), alpha_coef)


def reference(grad_field, alpha_coef, metric_inner, metric_outer):
    first = adjoint_pass(metric_inner[None, :, :, None] * grad_field, alpha_coef)
    padded = jnp.pad(first, ((0, 0), (1, 1), (0, 0), (0, 0)))
    smooth = first - 0.2 * (padded[:, 2:] - 2.0 * first + padded[:, :-2])
    middle = metric_outer[None, :, :, None] * smooth
    return adjoint_pass(middle, alpha_coef)
```

```python
import functools

import jax
import jax.numpy as jnp
from jax import lax
from jax.experimental import pallas as pl
from jax.experimental.pallas import tpu as pltpu
from jax.sharding import PartitionSpec as P

smooth_weight = 0.2
MESH = pl.DeviceIdType.MESH
f32, bf16 = jnp.float32, jnp.bfloat16
LANES = 128


def line_coefs(alpha):
    ratio = 2.0 * alpha / (1.0 + jnp.sqrt(1.0 - 4.0 * alpha * alpha))
    scale = (ratio / alpha) / (1.0 - ratio * ratio)
    near = 2.0 * (alpha + 2.0) / 3.0
    far = (4.0 * alpha - 1.0) / 3.0
    p, q = -ratio, -1.0 / ratio
    amp = -scale * (near * 0.5 * (p - q) + far * 0.25 * (p * p - q * q))
    delta = scale * far * 0.25 * (p - q)
    return jnp.stack([jnp.log(ratio), amp, delta])


def parity(n):
    return 1.0 - 2.0 * lax.rem(n, 2).astype(f32)


def kernel(
    bricks, peers, g_ref, coef, metric_in, metric_out, o_ref,
    gv, ov, zs, zr, tab, etab, load_sem, out_sem, zs_sem, zr_sem, xs_sem, xr_sem,
):
    fields, lines, cells, width = ov.shape
    b, d = lax.axis_index("brick"), lax.axis_index("gz")
    right, left = lax.rem(d + 1, peers), lax.rem(d + peers - 1, peers)
    has_low, has_high = b > 0, b < bricks - 1

    def load(f):
        return pltpu.make_async_copy(g_ref.at[f], gv.at[f, pl.ds(1, lines)], load_sem.at[f])

    def store(f):
        return pltpu.make_async_copy(ov.at[f], o_ref.at[f], out_sem.at[f])

    def z_copy(ps, way, f):
        return pltpu.make_async_remote_copy(
            src_ref=zs.at[ps, way, f], dst_ref=zr.at[ps, way, f],
            send_sem=zs_sem.at[ps, way, f], recv_sem=zr_sem.at[ps, way, f],
            device_id={"gz": right if way == 0 else left}, device_id_type=MESH,
        )

    def x_copy(way, f):
        src, dst, to = (1, lines + 1, b - 1) if way == 0 else (lines, 0, b + 1)
        return pltpu.make_async_remote_copy(
            src_ref=gv.at[f, src], dst_ref=gv.at[f, dst],
            send_sem=xs_sem.at[way, f], recv_sem=xr_sem.at[way, f],
            device_id={"brick": to}, device_id_type=MESH,
        )

    for f in range(fields):
        load(f).start()

    barrier = pltpu.get_barrier_semaphore()
    for z in (left, right):
        pl.semaphore_signal(barrier, inc=1, device_id={"gz": z}, device_id_type=MESH)

    @pl.when(has_low)
    def _():
        pl.semaphore_signal(barrier, inc=1, device_id={"brick": b - 1}, device_id_type=MESH)

    @pl.when(has_high)
    def _():
        pl.semaphore_signal(barrier, inc=1, device_id={"brick": b + 1}, device_id_type=MESH)

    rows = cells + 16
    i = lax.broadcasted_iota(jnp.int32, (rows, 2 * cells), 0)
    j = lax.rem(lax.broadcasted_iota(jnp.int32, (rows, 2 * cells), 1), cells)
    n = i - j
    main = i < cells
    to_right, to_left = i == cells, i == cells + 8
    dist = jnp.where(main, jnp.abs(n), jnp.where(to_right, cells - 1 - j, j))
    side = jnp.where(n > 0, 1.0, jnp.where(n < 0, -1.0, 0.0))
    tab[0] = dist.astype(f32)
    tab[1] = jnp.where(main, side, jnp.where(to_right | to_left, 1.0, 0.0)) * parity(dist)
    tab[2] = jnp.where(main & (dist == 1), side, 0.0)
    pick = ((i == cells + 1) & (j == cells - 1)) | ((i == cells + 9) & (j == 0))
    tab[3] = jnp.where(pick, 1.0, 0.0)
    ie = lax.broadcasted_iota(jnp.int32, (cells, LANES), 0)
    etab[0] = (ie + 1).astype(f32)
    etab[1] = parity(ie + 1)
    etab[2] = (cells - ie).astype(f32)
    etab[3] = -parity(cells - ie)

    @pl.when(jnp.logical_not(has_low))
    def _():
        gv[:, 0] = jnp.zeros((fields, cells, width), f32)

    @pl.when(jnp.logical_not(has_high))
    def _():
        gv[:, lines + 1] = jnp.zeros((fields, cells, width), f32)

    pl.semaphore_wait(barrier, 2 + has_low.astype(jnp.int32) + has_high.astype(jnp.int32))

    def product(f, x, metric, values):
        log_ratio = coef[0, f, pl.ds(x, 1), :]
        amp = coef[1, f, pl.ds(x, 1), :]
        delta = coef[2, f, pl.ds(x, 1), :]
        powers = tab[1] * jnp.exp(tab[0] * log_ratio)
        mat = jnp.concatenate([powers[:cells] * amp, powers[cells:]], axis=0)
        mat = (mat + tab[2] * delta + tab[3]) * metric[pl.ds(x, 1), :]
        high = mat.astype(bf16).astype(f32)
        column = lax.broadcasted_iota(jnp.int32, mat.shape, 1)
        split = jnp.where(column < cells, high, mat - high).astype(bf16)
        vh = values.astype(bf16)
        vl = (values - vh.astype(f32)).astype(bf16)
        return jnp.dot(
            jnp.concatenate([split, split], axis=1),
            jnp.concatenate([vh, vh, vl, vl], axis=0),
            preferred_element_type=f32,
        )

    def outgoing(ps, f, x, result):
        for kind in range(2):
            zs[ps, 0, f, kind, pl.ds(x, 1), :] = result[cells + kind : cells + kind + 1]
            zs[ps, 1, f, kind, pl.ds(x, 1), :] = result[cells + 8 + kind : cells + 9 + kind]

    def inner(f, x):
        result = product(f, x, metric_in, gv[f, x + 1])
        outgoing(0, f, x, result)
        gv[f, x + 1] = result[:cells]

    def outer(f, x):
        own = gv[f, x + 1]
        smooth = own - smooth_weight * (gv[f, x + 2] - 2.0 * own + gv[f, x])
        result = product(f, x, metric_out, smooth)
        outgoing(1, f, x, result)
        ov[f, x] = result[:cells]

    def finish(ps, f, x, ref, at):
        log_ratio = coef[0, f, pl.ds(x, 1), :]
        amp = coef[1, f, pl.ds(x, 1), :]
        delta = coef[2, f, pl.ds(x, 1), :]
        from_left = amp * etab[1] * jnp.exp(etab[0] * log_ratio)
        from_right = amp * etab[3] * jnp.exp(etab[2] * log_ratio)
        ie8 = lax.broadcasted_iota(jnp.int32, (8, LANES), 0)
        first8 = jnp.where(ie8 == 0, delta, 0.0)
        last8 = jnp.where(ie8 == 7, -delta, 0.0)
        low, high, low1, high1 = (
            zr[ps, way, f, kind, pl.ds(x, 1), :] for kind in range(2) for way in range(2)
        )
        for c in range(0, width, LANES):
            cols = slice(c, c + LANES)
            value = ref[f, at, :, cols] + from_left * low[:, cols] + from_right * high[:, cols]
            head = value[:8] + first8 * low1[:, cols]
            tail = value[cells - 8 :] + last8 * high1[:, cols]
            ref[f, at, :, cols] = jnp.concatenate([head, value[8 : cells - 8], tail], axis=0)

    def loop(low, high, body, unroll):
        def step(x, _):
            body(x)
            return 0

        lax.fori_loop(low, high, step, 0, unroll=unroll)

    lag = 2

    def first_pass(t):
        @pl.when(t < fields)
        def _():
            load(t).wait()
            loop(0, lines, lambda x: inner(t, x), 4)
            z_copy(0, 0, t).start()
            z_copy(0, 1, t).start()

        @pl.when(t >= lag)
        def _():
            f = t - lag
            z_copy(0, 0, f).wait_recv()
            z_copy(0, 1, f).wait_recv()
            finish(0, f, 0, gv, 1)
            finish(0, f, lines - 1, gv, lines)

            @pl.when(has_low)
            def _():
                x_copy(0, f).start()

            @pl.when(has_high)
            def _():
                x_copy(1, f).start()

            loop(1, lines - 1, lambda x: finish(0, f, x, gv, x + 1), 3)

    loop(0, fields + lag, first_pass, 1)
    loop(0, fields, lambda f: loop(1, lines - 1, lambda x: outer(f, x), 3), 1)

    def second_pass(t):
        @pl.when(t < fields)
        def _():
            @pl.when(has_high)
            def _():
                x_copy(0, t).wait_recv()

            @pl.when(has_low)
            def _():
                x_copy(1, t).wait_recv()

            outer(t, 0)
            outer(t, lines - 1)
            z_copy(1, 0, t).start()
            z_copy(1, 1, t).start()

        @pl.when(t >= 1)
        def _():
            f = t - 1
            z_copy(1, 0, f).wait_recv()
            z_copy(1, 1, f).wait_recv()
            loop(0, lines, lambda x: finish(1, f, x, ov, x), 4)
            store(f).start()

    loop(0, fields + 1, second_pass, 1)

    def drain(f):
        store(f).wait()
        for ps in range(2):
            for way in range(2):
                z_copy(ps, way, f).wait_send()

        @pl.when(has_low)
        def _():
            x_copy(0, f).wait_send()

        @pl.when(has_high)
        def _():
            x_copy(1, f).wait_send()

    loop(0, fields, drain, 1)


def body(bricks, peers, grad_field, alpha_coef, metric_inner, metric_outer):
    fields, lines, cells, width = grad_field.shape
    coef = jnp.broadcast_to(line_coefs(alpha_coef)[..., None], (3, fields, lines, LANES))
    twice = lambda m: jnp.concatenate([m, m], axis=1)
    dma = pltpu.SemaphoreType.DMA
    vmem = pl.BlockSpec(memory_space=pltpu.VMEM)
    return pl.pallas_call(
        functools.partial(kernel, bricks, peers),
        out_shape=jax.ShapeDtypeStruct(grad_field.shape, f32),
        in_specs=[pl.BlockSpec(memory_space=pl.ANY), vmem, vmem, vmem],
        out_specs=pl.BlockSpec(memory_space=pl.ANY),
        scratch_shapes=[
            pltpu.VMEM((fields, lines + 2, cells, width), f32),
            pltpu.VMEM((fields, lines, cells, width), f32),
            pltpu.VMEM((2, 2, fields, 2, lines, width), f32),
            pltpu.VMEM((2, 2, fields, 2, lines, width), f32),
            pltpu.VMEM((4, cells + 16, 2 * cells), f32),
            pltpu.VMEM((4, cells, LANES), f32),
            dma((fields,)), dma((fields,)),
            dma((2, 2, fields)), dma((2, 2, fields)), dma((2, fields)), dma((2, fields)),
        ],
        compiler_params=pltpu.CompilerParams(
            collective_id=0, has_side_effects=True, vmem_limit_bytes=40 * 1024 * 1024
        ),
    )(grad_field, coef, twice(metric_inner), twice(metric_outer))


def solution(mesh):
    placed = (P(None, "brick", "gz", None), P(None, "brick"), P("brick", "gz"), P("brick", "gz"))
    return jax.shard_map(
        functools.partial(body, mesh.shape["brick"], mesh.shape["gz"]),
        mesh=mesh, in_specs=placed, out_specs=P(None, "brick", "gz", None), check_vma=False,
    )
```

```python
import functools

import jax
import jax.numpy as jnp
from jax import lax
from jax.experimental import pallas as pl
from jax.experimental.pallas import tpu as pltpu
from jax.sharding import PartitionSpec as P

smooth_weight = 0.2
MESH = pl.DeviceIdType.MESH
f32, bf16 = jnp.float32, jnp.bfloat16
LANES = 128


def line_coefs(alpha):
    ratio = 2.0 * alpha / (1.0 + jnp.sqrt(1.0 - 4.0 * alpha * alpha))
    scale = (ratio / alpha) / (1.0 - ratio * ratio)
    near = 2.0 * (alpha + 2.0) / 3.0
    far = (4.0 * alpha - 1.0) / 3.0
    p, q = -ratio, -1.0 / ratio
    amp = -scale * (near * 0.5 * (p - q) + far * 0.25 * (p * p - q * q))
    delta = scale * far * 0.25 * (p - q)
    return jnp.log(ratio), amp, delta


def parity(n):
    return 1.0 - 2.0 * lax.rem(n, 2).astype(f32)


def kernel(
    bricks, peers, g_ref, alpha_ref, metric_in_ref, metric_out_ref, o_ref,
    gv, alpha_v, metric_v, metrics, coef, rb, zs, zr, es, er, tab, etab,
    small_sem, edge_sem, load_sem, zs_sem, zr_sem, es_sem, er_sem, xs_sem, xr_sem, rs_sem, rr_sem,
):
    fields, lines, cells, width = o_ref.shape
    b, d = lax.axis_index("brick"), lax.axis_index("gz")
    right, left = lax.rem(d + 1, peers), lax.rem(d + peers - 1, peers)
    has_low, has_high = b > 0, b < bricks - 1
    odd, core = lax.rem(b, 2), lax.rem(d, 2)
    paired = bricks % 2 == 0
    toward = 1 - 2 * odd
    last = lines - 1

    def local(src, dst, sem):
        return pltpu.make_async_copy(src, dst, sem)

    small = [
        local(alpha_ref, alpha_v, small_sem.at[0]),
        local(metric_in_ref, metric_v.at[0], small_sem.at[1]),
        local(metric_out_ref, metric_v.at[1], small_sem.at[2]),
    ]
    edges = [local(g_ref.at[:, x], gv.at[:, x + 1], edge_sem.at[k]) for k, x in enumerate((0, last))]

    def load(f):
        return local(g_ref.at[f, pl.ds(1, lines - 2)], gv.at[f, pl.ds(2, lines - 2)], load_sem.at[f])

    def remote(src, dst, send_sem, recv_sem, to):
        return pltpu.make_async_remote_copy(
            src_ref=src, dst_ref=dst, send_sem=send_sem, recv_sem=recv_sem,
            device_id=to, device_id_type=MESH,
        )

    def z_copy(ps, way, f):
        to = {"gz": right if way == 0 else left}
        return remote(zs.at[ps, way, f], zr.at[ps, way, f], zs_sem.at[ps, way, f], zr_sem.at[ps, way, f], to)

    def e_copy(ps, way, f):
        to = {"gz": right if way == 0 else left}
        return remote(es.at[ps, way, f], er.at[ps, way, f], es_sem.at[ps, way, f], er_sem.at[ps, way, f], to)

    def x_copy(way, f):
        src, dst, to = (1, lines + 1, b - 1) if way == 0 else (lines, 0, b + 1)
        return remote(gv.at[f, src], gv.at[f, dst], xs_sem.at[way, f], xr_sem.at[way, f], {"brick": to})

    def pair_copy(f):
        src = jnp.where(odd == 1, 1, lines)
        dst = jnp.where(odd == 1, lines + 1, 0)
        return remote(
            gv.at[f, src], gv.at[f, dst], xs_sem.at[0, f], xr_sem.at[1 - odd, f], {"brick": b + toward}
        )

    def hop_copy(f):
        src = jnp.where(odd == 1, lines, 1)
        to = jnp.where(core == 0, b + toward, b - 2 * toward)
        return remote(gv.at[f, src], rb.at[f], xs_sem.at[1, f], rr_sem.at[f], {"brick": to})

    def relay_copy(f):
        up = jnp.where(odd == core, 1, 0)
        dst = jnp.where(up == 1, 0, lines + 1)
        to = jnp.where(core == 0, b + 2 * toward, b + toward)
        return remote(rb.at[f], gv.at[f, dst], rs_sem.at[f], xr_sem.at[up, f], {"brick": to})

    hops = ((odd == 1) & has_high) | ((odd == 0) & has_low)
    relays = (b + 2 * toward >= 0) & (b + 2 * toward < bricks)

    def send_lines(f):
        if paired:
            @pl.when(hops)
            def _():
                hop_copy(f).start()

            pair_copy(f).start()
        else:
            @pl.when(has_low)
            def _():
                x_copy(0, f).start()

            @pl.when(has_high)
            def _():
                x_copy(1, f).start()

    def relay(f):
        if paired:
            @pl.when(relays)
            def _():
                hop_copy(f).wait_recv()
                relay_copy(f).start()

    def wait_lines(f):
        @pl.when(has_high)
        def _():
            x_copy(0, f).wait_recv()

        @pl.when(has_low)
        def _():
            x_copy(1, f).wait_recv()

    def lines_sent(f):
        if paired:
            pair_copy(f).wait_send()

            @pl.when(hops)
            def _():
                hop_copy(f).wait_send()

            @pl.when(relays)
            def _():
                relay_copy(f).wait_send()
        else:
            @pl.when(has_low)
            def _():
                x_copy(0, f).wait_send()

            @pl.when(has_high)
            def _():
                x_copy(1, f).wait_send()

    barrier = pltpu.get_barrier_semaphore()
    for z in (left, right):
        pl.semaphore_signal(barrier, inc=1, device_id={"gz": z}, device_id_type=MESH)
    expected = 2
    for step in (-2, -1, 1, 2):
        there = (b + step >= 0) & (b + step < bricks)
        expected = expected + jnp.where(there, 1, 0)

        @pl.when(there)
        def _():
            pl.semaphore_signal(barrier, inc=1, device_id={"brick": b + step}, device_id_type=MESH)

    for copy in small + edges:
        copy.start()
    for f in range(fields):
        load(f).start()

    rows = cells + 16
    i = lax.broadcasted_iota(jnp.int32, (rows, 2 * cells), 0)
    j = lax.rem(lax.broadcasted_iota(jnp.int32, (rows, 2 * cells), 1), cells)
    n = i - j
    main = i < cells
    to_right, to_left = i == cells, i == cells + 8
    dist = jnp.where(main, jnp.abs(n), jnp.where(to_right, cells - 1 - j, j))
    side = jnp.where(n > 0, 1.0, jnp.where(n < 0, -1.0, 0.0))
    tab[0] = dist.astype(f32)
    tab[1] = jnp.where(main, side, jnp.where(to_right | to_left, 1.0, 0.0)) * parity(dist)
    tab[2] = jnp.where(main & (dist == 1), side, 0.0)
    pick = ((i == cells + 1) & (j == cells - 1)) | ((i == cells + 9) & (j == 0))
    tab[3] = jnp.where(pick, 1.0, 0.0)
    ie = lax.broadcasted_iota(jnp.int32, (cells, LANES), 0)
    etab[0] = (ie + 1).astype(f32)
    etab[1] = parity(ie + 1)
    etab[2] = (cells - ie).astype(f32)
    etab[3] = -parity(cells - ie)

    @pl.when(jnp.logical_not(has_low))
    def _():
        gv[:, 0] = jnp.zeros((fields, cells, width), f32)

    @pl.when(jnp.logical_not(has_high))
    def _():
        gv[:, lines + 1] = jnp.zeros((fields, cells, width), f32)

    for copy in small:
        copy.wait()
    diagonal = lax.broadcasted_iota(jnp.int32, (lines, lines), 0) == lax.broadcasted_iota(
        jnp.int32, (lines, lines), 1
    )
    for k, values in enumerate(line_coefs(alpha_v[...])):
        for f in range(fields):
            column = jnp.sum(jnp.where(diagonal, values[f : f + 1], 0.0), axis=1, keepdims=True)
            coef[k, f] = jnp.broadcast_to(column, (lines, LANES))
    for k in range(2):
        metrics[k] = jnp.concatenate([metric_v[k], metric_v[k]], axis=1)

    def line_values(f, x):
        return (coef[k, f, pl.ds(x, 1), :] for k in range(3))

    def product(ps, f, x, values):
        log_ratio, amp, delta = line_values(f, x)
        powers = tab[1] * jnp.exp(tab[0] * log_ratio)
        mat = jnp.concatenate([powers[:cells] * amp, powers[cells:]], axis=0)
        mat = (mat + tab[2] * delta + tab[3]) * metrics[ps, pl.ds(x, 1), :]
        high = mat.astype(bf16).astype(f32)
        column = lax.broadcasted_iota(jnp.int32, mat.shape, 1)
        split = jnp.where(column < cells, high, mat - high).astype(bf16)
        vh = values.astype(bf16)
        vl = (values - vh.astype(f32)).astype(bf16)
        return jnp.dot(
            jnp.concatenate([split, split], axis=1),
            jnp.concatenate([vh, vh, vl, vl], axis=0),
            preferred_element_type=f32,
        )

    def outgoing(ps, f, x, result):
        edge = isinstance(x, int)
        for kind in range(2):
            for way in range(2):
                at = cells + 8 * way + kind
                row = result[at : at + 1]
                if edge:
                    at = 2 * kind + (x > 0)
                    es[ps, way, f, at : at + 1, :] = row
                else:
                    zs[ps, way, f, kind, pl.ds(x, 1), :] = row

    def inner(f, x):
        result = product(0, f, x, gv[f, x + 1])
        outgoing(0, f, x, result)
        gv[f, x + 1] = result[:cells]

    def outer(f, x):
        own = gv[f, x + 1]
        smooth = own - smooth_weight * (gv[f, x + 2] - 2.0 * own + gv[f, x])
        result = product(1, f, x, smooth)
        outgoing(1, f, x, result)
        o_ref[f, x] = result[:cells]

    def finish(ps, f, x):
        ref, line = (gv, x + 1) if ps == 0 else (o_ref, x)
        log_ratio, amp, delta = line_values(f, x)
        from_left = amp * etab[1] * jnp.exp(etab[0] * log_ratio)
        from_right = amp * etab[3] * jnp.exp(etab[2] * log_ratio)
        ie8 = lax.broadcasted_iota(jnp.int32, (8, LANES), 0)
        first8 = jnp.where(ie8 == 0, delta, 0.0)
        last8 = jnp.where(ie8 == 7, -delta, 0.0)
        if isinstance(x, int):
            at = int(x > 0)
            low, high, low1, high1 = (
                er[ps, way, f, 2 * kind + at : 2 * kind + at + 1, :] for kind in range(2) for way in range(2)
            )
        else:
            low, high, low1, high1 = (
                zr[ps, way, f, kind, pl.ds(x, 1), :] for kind in range(2) for way in range(2)
            )
        for c in range(0, width, LANES):
            cols = slice(c, c + LANES)
            value = ref[f, line, :, cols] + from_left * low[:, cols] + from_right * high[:, cols]
            head = value[:8] + first8 * low1[:, cols]
            tail = value[cells - 8 :] + last8 * high1[:, cols]
            ref[f, line, :, cols] = jnp.concatenate([head, value[8 : cells - 8], tail], axis=0)

    def loop(low, high, body, unroll=1):
        def step(x, _):
            body(x)
            return 0

        lax.fori_loop(low, high, step, 0, unroll=unroll)

    def both(copy, ps, f, act):
        for way in range(2):
            getattr(copy(ps, way, f), act)()

    pl.semaphore_wait(barrier, expected)
    for copy in edges:
        copy.wait()

    def edges_in(f):
        inner(f, 0)
        inner(f, last)
        both(e_copy, 0, f, "start")

    def inside_in(f):
        load(f).wait()
        loop(1, last, lambda x: inner(f, x), 3)
        both(z_copy, 0, f, "start")

    def edges_first(f):
        both(e_copy, 0, f, "wait_recv")
        finish(0, f, 0)
        finish(0, f, last)
        send_lines(f)

    def inside_first(f):
        both(z_copy, 0, f, "wait_recv")
        loop(1, last, lambda x: finish(0, f, x), 3)

    def inside_out(f):
        loop(1, last, lambda x: outer(f, x), 3)
        both(z_copy, 1, f, "start")

    def inside_last(f):
        both(z_copy, 1, f, "wait_recv")
        loop(1, last, lambda x: finish(1, f, x), 3)

    loop(0, fields, edges_in)
    inside_in(0)
    loop(0, fields, edges_first)
    loop(1, fields, inside_in)
    loop(0, fields, inside_first)
    relay(0)
    loop(0, fields, inside_out)
    loop(0, fields, inside_last)

    def edges_last(t):
        @pl.when(t + 1 < fields)
        def _():
            relay(t + 1)

        @pl.when(t < fields)
        def _():
            wait_lines(t)
            outer(t, 0)
            outer(t, last)
            both(e_copy, 1, t, "start")

        @pl.when(t >= 1)
        def _():
            f = t - 1
            both(e_copy, 1, f, "wait_recv")
            finish(1, f, 0)
            finish(1, f, last)

    loop(0, fields + 1, edges_last)

    def drain(f):
        for ps in range(2):
            both(z_copy, ps, f, "wait_send")
            both(e_copy, ps, f, "wait_send")
        lines_sent(f)

    loop(0, fields, drain)


def body(bricks, peers, grad_field, alpha_coef, metric_inner, metric_outer):
    fields, lines, cells, width = grad_field.shape
    dma = pltpu.SemaphoreType.DMA
    far = pl.BlockSpec(memory_space=pltpu.HBM)
    return pl.pallas_call(
        functools.partial(kernel, bricks, peers),
        out_shape=jax.ShapeDtypeStruct(grad_field.shape, f32),
        in_specs=[far] * 4,
        out_specs=pl.BlockSpec(memory_space=pltpu.VMEM),
        scratch_shapes=[
            pltpu.VMEM((fields, lines + 2, cells, width), f32),
            pltpu.VMEM((fields, lines), f32),
            pltpu.VMEM((2, lines, cells), f32),
            pltpu.VMEM((2, lines, 2 * cells), f32),
            pltpu.VMEM((3, fields, lines, LANES), f32),
            pltpu.VMEM((fields, cells, width), f32),
            pltpu.VMEM((2, 2, fields, 2, lines, width), f32),
            pltpu.VMEM((2, 2, fields, 2, lines, width), f32),
            pltpu.VMEM((2, 2, fields, 8, width), f32),
            pltpu.VMEM((2, 2, fields, 8, width), f32),
            pltpu.VMEM((4, cells + 16, 2 * cells), f32),
            pltpu.VMEM((4, cells, LANES), f32),
            dma((3,)), dma((2,)), dma((fields,)),
            dma((2, 2, fields)), dma((2, 2, fields)), dma((2, 2, fields)), dma((2, 2, fields)),
            dma((2, fields)), dma((2, fields)), dma((fields,)), dma((fields,)),
        ],
        compiler_params=pltpu.CompilerParams(
            collective_id=0, has_side_effects=True, vmem_limit_bytes=40 * 1024 * 1024
        ),
    )(*(pltpu.with_memory_space_constraint(a, pltpu.HBM) for a in (grad_field, alpha_coef, metric_inner, metric_outer)))


def solution(mesh):
    placed = (P(None, "brick", "gz", None), P(None, "brick"), P("brick", "gz"), P("brick", "gz"))
    return jax.shard_map(
        functools.partial(body, mesh.shape["brick"], mesh.shape["gz"]),
        mesh=mesh, in_specs=placed, out_specs=P(None, "brick", "gz", None), check_vma=False,
    )
```

```python
import functools

import jax
import jax.numpy as jnp
from jax import lax
from jax.experimental import pallas as pl
from jax.experimental.pallas import tpu as pltpu
from jax.sharding import PartitionSpec as P

smooth_weight = 0.2
MESH = pl.DeviceIdType.MESH
f32, bf16 = jnp.float32, jnp.bfloat16
LANES = 128


def line_coefs(alpha):
    ratio = 2.0 * alpha / (1.0 + jnp.sqrt(1.0 - 4.0 * alpha * alpha))
    scale = (ratio / alpha) / (1.0 - ratio * ratio)
    near = 2.0 * (alpha + 2.0) / 3.0
    far = (4.0 * alpha - 1.0) / 3.0
    p, q = -ratio, -1.0 / ratio
    amp = -scale * (near * 0.5 * (p - q) + far * 0.25 * (p * p - q * q))
    delta = scale * far * 0.25 * (p - q)
    return jnp.log(ratio), amp, delta


def parity(n):
    return 1.0 - 2.0 * lax.rem(n, 2).astype(f32)


def kernel(
    bricks, peers, early, g_ref, alpha_ref, metric_in_ref, metric_out_ref, o_ref,
    gv, alpha_v, metric_v, alpha_n, metric_n, metrics, coef, rb, zs, zr, es, er, hx, tab, etab,
    ns_sem, nr_sem, hs_sem, hr_sem, small_sem, edge_sem, load_sem, zs_sem, zr_sem, es_sem, er_sem, xs_sem, xr_sem, rs_sem, rr_sem,
):
    fields, lines, cells, width = o_ref.shape
    b, d = lax.axis_index("brick"), lax.axis_index("gz")
    right, left = lax.rem(d + 1, peers), lax.rem(d + peers - 1, peers)
    has_low, has_high = b > 0, b < bricks - 1
    odd, core = lax.rem(b, 2), lax.rem(d, 2)
    paired = bricks % 2 == 0
    toward = 1 - 2 * odd
    last = lines - 1

    def local(src, dst, sem):
        return pltpu.make_async_copy(src, dst, sem)

    small = [
        local(alpha_ref, alpha_v, small_sem.at[0]),
        local(metric_in_ref, metric_v.at[0], small_sem.at[1]),
        local(metric_out_ref, metric_v.at[1], small_sem.at[2]),
    ]
    edges = [local(g_ref.at[:, x], gv.at[:, x + 1], edge_sem.at[k]) for k, x in enumerate((0, last))]

    def load(f):
        return local(g_ref.at[f, pl.ds(1, lines - 2)], gv.at[f, pl.ds(2, lines - 2)], load_sem.at[f])

    def remote(src, dst, send_sem, recv_sem, to):
        return pltpu.make_async_remote_copy(
            src_ref=src, dst_ref=dst, send_sem=send_sem, recv_sem=recv_sem,
            device_id=to, device_id_type=MESH,
        )

    def z_copy(ps, way, f):
        to = {"gz": right if way == 0 else left}
        return remote(zs.at[ps, way, f], zr.at[ps, way, f], zs_sem.at[ps, way, f], zr_sem.at[ps, way, f], to)

    def e_copy(ps, way, f):
        to = {"gz": right if way == 0 else left}
        return remote(es.at[ps, f, :, way], er.at[ps, f, :, way], es_sem.at[ps, way, f], er_sem.at[ps, way, f], to)

    def x_copy(way, f, raw=False):
        src, dst, to = (0, lines + 1, b - 1) if way == 0 else (last, 0, b + 1)
        return remote(line_of(f, src, raw), gv.at[f, dst], xs_sem.at[way, f], xr_sem.at[way, f], {"brick": to})

    def line_of(f, index, raw):
        return g_ref.at[f, index] if raw else gv.at[f, index + 1]

    def pair_copy(f, raw=False):
        src = line_of(f, jnp.where(odd == 1, 0, last), raw)
        dst = jnp.where(odd == 1, lines + 1, 0)
        return remote(
            src, gv.at[f, dst], xs_sem.at[0, f], xr_sem.at[1 - odd, f], {"brick": b + toward}
        )

    def hop_copy(f, raw=False):
        src = line_of(f, jnp.where(odd == 1, last, 0), raw)
        to = jnp.where(core == 0, b + toward, b - 2 * toward)
        return remote(src, rb.at[f], xs_sem.at[1, f], rr_sem.at[f], {"brick": to})

    def relay_copy(f):
        up = jnp.where(odd == core, 1, 0)
        dst = jnp.where(up == 1, 0, lines + 1)
        to = jnp.where(core == 0, b + 2 * toward, b + toward)
        return remote(rb.at[f], gv.at[f, dst], rs_sem.at[f], xr_sem.at[up, f], {"brick": to})

    hops = ((odd == 1) & has_high) | ((odd == 0) & has_low)
    relays = (b + 2 * toward >= 0) & (b + 2 * toward < bricks)

    def send_lines(f, raw=False):
        if paired:
            @pl.when(hops)
            def _():
                hop_copy(f, raw).start()

            pair_copy(f, raw).start()
        else:
            @pl.when(has_low)
            def _():
                x_copy(0, f, raw).start()

            @pl.when(has_high)
            def _():
                x_copy(1, f, raw).start()

    def beside(way):
        return {"brick": b - 1 if way == 0 else b + 1}

    def neighbour_copies(way):
        return [
            remote(src, dst.at[1 - way], ns_sem.at[way, k], nr_sem.at[way, k], beside(way))
            for k, (src, dst) in enumerate(((alpha_ref, alpha_n), (metric_in_ref, metric_n)))
        ]

    def row_copy(way, f):
        return remote(er.at[0, f, way], hx.at[f, 1 - way], hs_sem.at[way, f], hr_sem.at[way, f], beside(way))

    def relay(f):
        if paired:
            @pl.when(relays)
            def _():
                hop_copy(f).wait_recv()
                relay_copy(f).start()

    def wait_lines(f):
        @pl.when(has_high)
        def _():
            x_copy(0, f).wait_recv()

        @pl.when(has_low)
        def _():
            x_copy(1, f).wait_recv()

    def lines_sent(f):
        if paired:
            pair_copy(f).wait_send()

            @pl.when(hops)
            def _():
                hop_copy(f).wait_send()

            @pl.when(relays)
            def _():
                relay_copy(f).wait_send()
        else:
            @pl.when(has_low)
            def _():
                x_copy(0, f).wait_send()

            @pl.when(has_high)
            def _():
                x_copy(1, f).wait_send()

    barrier = pltpu.get_barrier_semaphore()
    for z in (left, right):
        pl.semaphore_signal(barrier, inc=1, device_id={"gz": z}, device_id_type=MESH)
    expected = 2
    for step in (-2, -1, 1, 2):
        there = (b + step >= 0) & (b + step < bricks)
        expected = expected + jnp.where(there, 1, 0)

        @pl.when(there)
        def _():
            pl.semaphore_signal(barrier, inc=1, device_id={"brick": b + step}, device_id_type=MESH)

    for copy in small + edges:
        copy.start()
    for f in range(fields):
        load(f).start()

    pl.semaphore_wait(barrier, expected)
    for f in range(early):
        send_lines(f, True)
    for way, there in enumerate((has_low, has_high)):
        @pl.when(there)
        def _():
            for copy in neighbour_copies(way):
                copy.start()

    rows = cells + 16
    i = lax.broadcasted_iota(jnp.int32, (rows, 2 * cells), 0)
    j = lax.rem(lax.broadcasted_iota(jnp.int32, (rows, 2 * cells), 1), cells)
    n = i - j
    main = i < cells
    to_right, to_left = i == cells, i == cells + 8
    dist = jnp.where(main, jnp.abs(n), jnp.where(to_right, cells - 1 - j, j))
    side = jnp.where(n > 0, 1.0, jnp.where(n < 0, -1.0, 0.0))
    tab[0] = dist.astype(f32)
    tab[1] = jnp.where(main, side, jnp.where(to_right | to_left, 1.0, 0.0)) * parity(dist)
    tab[2] = jnp.where(main & (dist == 1), side, 0.0)
    pick = ((i == cells + 1) & (j == cells - 1)) | ((i == cells + 9) & (j == 0))
    tab[3] = jnp.where(pick, 1.0, 0.0)
    ie = lax.broadcasted_iota(jnp.int32, (cells, LANES), 0)
    etab[0] = (ie + 1).astype(f32)
    etab[1] = parity(ie + 1)
    etab[2] = (cells - ie).astype(f32)
    etab[3] = -parity(cells - ie)

    @pl.when(jnp.logical_not(has_low))
    def _():
        gv[:, 0] = jnp.zeros((fields, cells, width), f32)

    @pl.when(jnp.logical_not(has_high))
    def _():
        gv[:, lines + 1] = jnp.zeros((fields, cells, width), f32)

    for copy in small:
        copy.wait()
    diagonal = lax.broadcasted_iota(jnp.int32, (lines, lines), 0) == lax.broadcasted_iota(
        jnp.int32, (lines, lines), 1
    )
    for k, values in enumerate(line_coefs(alpha_v[...])):
        for f in range(fields):
            column = jnp.sum(jnp.where(diagonal, values[f : f + 1], 0.0), axis=1, keepdims=True)
            coef[k, f, :lines] = jnp.broadcast_to(column, (lines, LANES))
    for k in range(2):
        metrics[k, :lines] = jnp.concatenate([metric_v[k], metric_v[k]], axis=1)

    def line_values(f, x):
        return (coef[k, f, pl.ds(x, 1), :] for k in range(3))

    def product(ps, f, x, values):
        log_ratio, amp, delta = line_values(f, x)
        powers = tab[1] * jnp.exp(tab[0] * log_ratio)
        mat = jnp.concatenate([powers[:cells] * amp, powers[cells:]], axis=0)
        mat = (mat + tab[2] * delta + tab[3]) * metrics[ps, pl.ds(x, 1), :]
        high = mat.astype(bf16).astype(f32)
        column = lax.broadcasted_iota(jnp.int32, mat.shape, 1)
        split = jnp.where(column < cells, high, mat - high).astype(bf16)
        vh = values.astype(bf16)
        vl = (values - vh.astype(f32)).astype(bf16)
        return jnp.dot(
            jnp.concatenate([split, split], axis=1),
            jnp.concatenate([vh, vh, vl, vl], axis=0),
            preferred_element_type=f32,
        )

    def outgoing(ps, f, x, result):
        edge = isinstance(x, int)
        for kind in range(2):
            for way in range(2):
                at = cells + 8 * way + kind
                row = result[at : at + 1]
                if edge:
                    es[ps, f, int(x > 0), way, kind : kind + 1, :] = row
                else:
                    zs[ps, way, f, kind, pl.ds(x, 1), :] = row

    def inner(f, x):
        result = product(0, f, x, gv[f, x + 1])
        outgoing(0, f, x, result)
        gv[f, x + 1] = result[:cells]

    def outer(f, x):
        own = gv[f, x + 1]
        smooth = own - smooth_weight * (gv[f, x + 2] - 2.0 * own + gv[f, x])
        result = product(1, f, x, smooth)
        outgoing(1, f, x, result)
        o_ref[f, x] = result[:cells]

    def finish(ps, f, x, halo=None):
        ref, line = (gv, x + 1) if ps == 0 else (o_ref, x)
        if halo is not None:
            line = halo * (lines + 1)
        log_ratio, amp, delta = line_values(f, x)
        from_left = amp * etab[1] * jnp.exp(etab[0] * log_ratio)
        from_right = amp * etab[3] * jnp.exp(etab[2] * log_ratio)
        ie8 = lax.broadcasted_iota(jnp.int32, (8, LANES), 0)
        first8 = jnp.where(ie8 == 0, delta, 0.0)
        last8 = jnp.where(ie8 == 7, -delta, 0.0)
        if isinstance(x, int):
            rows = er.at[ps, f, int(x > 0)] if halo is None else hx.at[f, halo]
            low, high, low1, high1 = (
                rows[way, kind : kind + 1, :] for kind in range(2) for way in range(2)
            )
        else:
            low, high, low1, high1 = (
                zr[ps, way, f, kind, pl.ds(x, 1), :] for kind in range(2) for way in range(2)
            )
        for c in range(0, width, LANES):
            cols = slice(c, c + LANES)
            value = ref[f, line, :, cols] + from_left * low[:, cols] + from_right * high[:, cols]
            head = value[:8] + first8 * low1[:, cols]
            tail = value[cells - 8 :] + last8 * high1[:, cols]
            ref[f, line, :, cols] = jnp.concatenate([head, value[8 : cells - 8], tail], axis=0)

    def loop(low, high, body, unroll=1):
        def step(x, _):
            body(x)
            return 0

        lax.fori_loop(low, high, step, 0, unroll=unroll)

    def both(copy, ps, f, act):
        for way in range(2):
            getattr(copy(ps, way, f), act)()

    for copy in edges:
        copy.wait()

    def edges_in(f):
        inner(f, 0)
        inner(f, last)
        both(e_copy, 0, f, "start")

    def inside_in(f):
        load(f).wait()
        loop(1, last, lambda x: inner(f, x), 3)
        both(z_copy, 0, f, "start")

    def edges_first(f):
        both(e_copy, 0, f, "wait_recv")
        finish(0, f, 0)
        finish(0, f, last)

        @pl.when(f >= early)
        def _():
            send_lines(f)

        @pl.when(f < early)
        def _():
            for way, there in enumerate((has_low, has_high)):
                @pl.when(there)
                def _():
                    row_copy(way, f).start()

    def inside_first(f):
        both(z_copy, 0, f, "wait_recv")
        loop(1, last, lambda x: finish(0, f, x), 3)

    def inside_out(f):
        loop(1, last, lambda x: outer(f, x), 3)
        both(z_copy, 1, f, "start")

    def inside_last(f):
        both(z_copy, 1, f, "wait_recv")
        loop(1, last, lambda x: finish(1, f, x), 3)

    loop(0, fields, edges_in)
    inside_in(0)
    loop(0, fields, edges_first)
    loop(1, fields, inside_in)
    loop(0, fields, inside_first)
    relay(0)
    loop(0, fields, inside_out)
    loop(0, fields, inside_last)

    def halo_ready(side):
        for copy in neighbour_copies(1 - side):
            copy.wait_recv()
        line, row = (last, lines) if side == 0 else (0, lines + 1)
        for k, values in enumerate(line_coefs(alpha_n[side])):
            for f in range(early):
                coef[k, f, row : row + 1] = jnp.broadcast_to(values[f : f + 1, line : line + 1], (1, LANES))
        values = metric_n[side, line : line + 1, :]
        metrics[0, row : row + 1] = jnp.concatenate([values, values], axis=1)

    def halo_first(f, side):
        row_copy(1 - side, f).wait_recv()
        line = side * (lines + 1)
        gv[f, line] = product(0, f, lines + side, gv[f, line])[:cells]
        finish(0, f, lines + side, side)

    for side, there in enumerate((has_low, has_high)):
        @pl.when(there)
        def _():
            halo_ready(side)

    def edges_last(t):
        @pl.when(t + 1 < fields)
        def _():
            relay(t + 1)

        @pl.when(t < fields)
        def _():
            wait_lines(t)

            @pl.when(t < early)
            def _():
                for side, there in enumerate((has_low, has_high)):
                    @pl.when(there)
                    def _():
                        halo_first(t, side)

            outer(t, 0)
            outer(t, last)
            both(e_copy, 1, t, "start")

        @pl.when(t >= 1)
        def _():
            f = t - 1
            both(e_copy, 1, f, "wait_recv")
            finish(1, f, 0)
            finish(1, f, last)

    loop(0, fields + 1, edges_last)

    def drain(f):
        for ps in range(2):
            both(z_copy, ps, f, "wait_send")
            both(e_copy, ps, f, "wait_send")
        lines_sent(f)

    loop(0, fields, drain)
    for way, there in enumerate((has_low, has_high)):
        @pl.when(there)
        def _():
            for copy in neighbour_copies(way):
                copy.wait_send()
            for f in range(early):
                row_copy(way, f).wait_send()


def body(bricks, peers, grad_field, alpha_coef, metric_inner, metric_outer):
    fields, lines, cells, width = grad_field.shape
    dma = pltpu.SemaphoreType.DMA
    early = min(2, fields)
    far = pl.BlockSpec(memory_space=pltpu.HBM)
    return pl.pallas_call(
        functools.partial(kernel, bricks, peers, early),
        out_shape=jax.ShapeDtypeStruct(grad_field.shape, f32),
        in_specs=[far] * 4,
        out_specs=pl.BlockSpec(memory_space=pltpu.VMEM),
        scratch_shapes=[
            pltpu.VMEM((fields, lines + 2, cells, width), f32),
            pltpu.VMEM((fields, lines), f32),
            pltpu.VMEM((2, lines, cells), f32),
            pltpu.VMEM((2, fields, lines), f32),
            pltpu.VMEM((2, lines, cells), f32),
            pltpu.VMEM((2, lines + 8, 2 * cells), f32),
            pltpu.VMEM((3, fields, lines + 8, LANES), f32),
            pltpu.VMEM((fields, cells, width), f32),
            pltpu.VMEM((2, 2, fields, 2, lines, width), f32),
            pltpu.VMEM((2, 2, fields, 2, lines, width), f32),
            pltpu.VMEM((2, fields, 2, 2, 2, width), f32),
            pltpu.VMEM((2, fields, 2, 2, 2, width), f32),
            pltpu.VMEM((early, 2, 2, 2, width), f32),
            pltpu.VMEM((4, cells + 16, 2 * cells), f32),
            pltpu.VMEM((4, cells, LANES), f32),
            dma((2, 2)), dma((2, 2)), dma((2, early)), dma((2, early)),
            dma((3,)), dma((2,)), dma((fields,)),
            dma((2, 2, fields)), dma((2, 2, fields)), dma((2, 2, fields)), dma((2, 2, fields)),
            dma((2, fields)), dma((2, fields)), dma((fields,)), dma((fields,)),
        ],
        compiler_params=pltpu.CompilerParams(
            collective_id=0, has_side_effects=True, vmem_limit_bytes=40 * 1024 * 1024
        ),
    )(*(pltpu.with_memory_space_constraint(a, pltpu.HBM) for a in (grad_field, alpha_coef, metric_inner, metric_outer)))


def solution(mesh):
    placed = (P(None, "brick", "gz", None), P(None, "brick"), P("brick", "gz"), P("brick", "gz"))
    return jax.shard_map(
        functools.partial(body, mesh.shape["brick"], mesh.shape["gz"]),
        mesh=mesh, in_specs=placed, out_specs=P(None, "brick", "gz", None), check_vma=False,
    )
```

```python
import functools

import jax
import jax.numpy as jnp
from jax import lax
from jax.experimental import pallas as pl
from jax.experimental.pallas import tpu as pltpu
from jax.sharding import PartitionSpec as P

smooth_weight = 0.2
MESH = pl.DeviceIdType.MESH
f32, bf16 = jnp.float32, jnp.bfloat16
LANES = 128


def line_coefs(alpha):
    ratio = 2.0 * alpha / (1.0 + jnp.sqrt(1.0 - 4.0 * alpha * alpha))
    scale = (ratio / alpha) / (1.0 - ratio * ratio)
    near = 2.0 * (alpha + 2.0) / 3.0
    far = (4.0 * alpha - 1.0) / 3.0
    p, q = -ratio, -1.0 / ratio
    amp = -scale * (near * 0.5 * (p - q) + far * 0.25 * (p * p - q * q))
    delta = scale * far * 0.25 * (p - q)
    return jnp.log(ratio), amp, delta


def parity(n):
    return 1.0 - 2.0 * lax.rem(n, 2).astype(f32)


def kernel(
    bricks, peers, early, g_ref, alpha_ref, metric_in_ref, metric_out_ref, o_ref,
    gv, alpha_v, metric_v, alpha_n, metric_n, metrics, coef, rb, zs, zr, es, er, hx, tab, etab, mats, weights,
    ns_sem, nr_sem, hs_sem, hr_sem, small_sem, edge_sem, load_sem, zs_sem, zr_sem, es_sem, er_sem, xs_sem, xr_sem, rs_sem, rr_sem,
):
    fields, lines, cells, width = o_ref.shape
    b, d = lax.axis_index("brick"), lax.axis_index("gz")
    right, left = lax.rem(d + 1, peers), lax.rem(d + peers - 1, peers)
    has_low, has_high = b > 0, b < bricks - 1
    odd, core = lax.rem(b, 2), lax.rem(d, 2)
    paired = bricks % 2 == 0
    toward = 1 - 2 * odd
    last = lines - 1

    def local(src, dst, sem):
        return pltpu.make_async_copy(src, dst, sem)

    small = [
        local(alpha_ref, alpha_v, small_sem.at[0]),
        local(metric_in_ref, metric_v.at[0], small_sem.at[1]),
        local(metric_out_ref, metric_v.at[1], small_sem.at[2]),
    ]
    edges = [local(g_ref.at[:, x], gv.at[:, x + 1], edge_sem.at[k]) for k, x in enumerate((0, last))]

    def load(f):
        return local(g_ref.at[f, pl.ds(1, lines - 2)], gv.at[f, pl.ds(2, lines - 2)], load_sem.at[f])

    def remote(src, dst, send_sem, recv_sem, to):
        return pltpu.make_async_remote_copy(
            src_ref=src, dst_ref=dst, send_sem=send_sem, recv_sem=recv_sem,
            device_id=to, device_id_type=MESH,
        )

    def z_copy(ps, way, f):
        to = {"gz": right if way == 0 else left}
        return remote(zs.at[ps, way, f], zr.at[ps, way, f], zs_sem.at[ps, way, f], zr_sem.at[ps, way, f], to)

    def e_copy(ps, way, f):
        to = {"gz": right if way == 0 else left}
        return remote(es.at[ps, f, :, way], er.at[ps, f, :, way], es_sem.at[ps, way, f], er_sem.at[ps, way, f], to)

    def x_copy(way, f, raw=False):
        src, dst, to = (0, lines + 1, b - 1) if way == 0 else (last, 0, b + 1)
        return remote(line_of(f, src, raw), gv.at[f, dst], xs_sem.at[way, f], xr_sem.at[way, f], {"brick": to})

    def line_of(f, index, raw):
        return g_ref.at[f, index] if raw else gv.at[f, index + 1]

    def pair_copy(f, raw=False):
        src = line_of(f, jnp.where(odd == 1, 0, last), raw)
        dst = jnp.where(odd == 1, lines + 1, 0)
        return remote(
            src, gv.at[f, dst], xs_sem.at[0, f], xr_sem.at[1 - odd, f], {"brick": b + toward}
        )

    def hop_copy(f, raw=False):
        src = line_of(f, jnp.where(odd == 1, last, 0), raw)
        to = jnp.where(core == 0, b + toward, b - 2 * toward)
        return remote(src, rb.at[f], xs_sem.at[1, f], rr_sem.at[f], {"brick": to})

    def relay_copy(f):
        up = jnp.where(odd == core, 1, 0)
        dst = jnp.where(up == 1, 0, lines + 1)
        to = jnp.where(core == 0, b + 2 * toward, b + toward)
        return remote(rb.at[f], gv.at[f, dst], rs_sem.at[f], xr_sem.at[up, f], {"brick": to})

    hops = ((odd == 1) & has_high) | ((odd == 0) & has_low)
    relays = (b + 2 * toward >= 0) & (b + 2 * toward < bricks)

    def send_lines(f, raw=False):
        if paired:
            @pl.when(hops)
            def _():
                hop_copy(f, raw).start()

            pair_copy(f, raw).start()
        else:
            @pl.when(has_low)
            def _():
                x_copy(0, f, raw).start()

            @pl.when(has_high)
            def _():
                x_copy(1, f, raw).start()

    def beside(way):
        return {"brick": b - 1 if way == 0 else b + 1}

    def neighbour_copies(way):
        return [
            remote(src, dst.at[1 - way], ns_sem.at[way, k], nr_sem.at[way, k], beside(way))
            for k, (src, dst) in enumerate(((alpha_ref, alpha_n), (metric_in_ref, metric_n)))
        ]

    def row_copy(way, f):
        return remote(er.at[0, f, way], hx.at[f, 1 - way], hs_sem.at[way, f], hr_sem.at[way, f], beside(way))

    def relay(f):
        if paired:
            @pl.when(relays)
            def _():
                hop_copy(f).wait_recv()
                relay_copy(f).start()

    def wait_lines(f):
        @pl.when(has_high)
        def _():
            x_copy(0, f).wait_recv()

        @pl.when(has_low)
        def _():
            x_copy(1, f).wait_recv()

    def lines_sent(f):
        if paired:
            pair_copy(f).wait_send()

            @pl.when(hops)
            def _():
                hop_copy(f).wait_send()

            @pl.when(relays)
            def _():
                relay_copy(f).wait_send()
        else:
            @pl.when(has_low)
            def _():
                x_copy(0, f).wait_send()

            @pl.when(has_high)
            def _():
                x_copy(1, f).wait_send()

    barrier = pltpu.get_barrier_semaphore()
    for z in (left, right):
        pl.semaphore_signal(barrier, inc=1, device_id={"gz": z}, device_id_type=MESH)
    expected = 2
    for step in (-2, -1, 1, 2):
        there = (b + step >= 0) & (b + step < bricks)
        expected = expected + jnp.where(there, 1, 0)

        @pl.when(there)
        def _():
            pl.semaphore_signal(barrier, inc=1, device_id={"brick": b + step}, device_id_type=MESH)

    for copy in small + edges:
        copy.start()
    for f in range(fields):
        load(f).start()

    pl.semaphore_wait(barrier, expected)
    for f in range(early):
        send_lines(f, True)
    for way, there in enumerate((has_low, has_high)):
        @pl.when(there)
        def _():
            for copy in neighbour_copies(way):
                copy.start()

    rows = cells + 16
    i = lax.broadcasted_iota(jnp.int32, (rows, 2 * cells), 0)
    j = lax.rem(lax.broadcasted_iota(jnp.int32, (rows, 2 * cells), 1), cells)
    n = i - j
    main = i < cells
    to_right, to_left = i == cells, i == cells + 8
    dist = jnp.where(main, jnp.abs(n), jnp.where(to_right, cells - 1 - j, j))
    side = jnp.where(n > 0, 1.0, jnp.where(n < 0, -1.0, 0.0))
    tab[0] = dist.astype(f32)
    tab[1] = jnp.where(main, side, jnp.where(to_right | to_left, 1.0, 0.0)) * parity(dist)
    tab[2] = jnp.where(main & (dist == 1), side, 0.0)
    pick = ((i == cells + 1) & (j == cells - 1)) | ((i == cells + 9) & (j == 0))
    tab[3] = jnp.where(pick, 1.0, 0.0)
    ie = lax.broadcasted_iota(jnp.int32, (cells, LANES), 0)
    etab[0] = (ie + 1).astype(f32)
    etab[1] = parity(ie + 1)
    etab[2] = (cells - ie).astype(f32)
    etab[3] = -parity(cells - ie)

    @pl.when(jnp.logical_not(has_low))
    def _():
        gv[:, 0] = jnp.zeros((fields, cells, width), f32)

    @pl.when(jnp.logical_not(has_high))
    def _():
        gv[:, lines + 1] = jnp.zeros((fields, cells, width), f32)

    for copy in small:
        copy.wait()
    diagonal = lax.broadcasted_iota(jnp.int32, (lines, lines), 0) == lax.broadcasted_iota(
        jnp.int32, (lines, lines), 1
    )
    for k, values in enumerate(line_coefs(alpha_v[...])):
        for f in range(fields):
            column = jnp.sum(jnp.where(diagonal, values[f : f + 1], 0.0), axis=1, keepdims=True)
            coef[k, f, :lines] = jnp.broadcast_to(column, (lines, LANES))
    for k in range(2):
        metrics[k, :lines] = jnp.concatenate([metric_v[k], metric_v[k]], axis=1)

    def line_values(f, x):
        return (coef[k, f, pl.ds(x, 1), :] for k in range(3))

    def product(ps, f, x, values, keep=True):
        if ps == 0:
            log_ratio, amp, delta = line_values(f, x)
            powers = tab[1] * jnp.exp(tab[0] * log_ratio)
            mat = jnp.concatenate([powers[:cells] * amp, powers[cells:]], axis=0)
            mat = mat + tab[2] * delta + tab[3]
            if keep:
                mats[f, x] = mat
        else:
            mat = mats[f, x]
        mat = mat * metrics[ps, pl.ds(x, 1), :]
        high = mat.astype(bf16).astype(f32)
        column = lax.broadcasted_iota(jnp.int32, mat.shape, 1)
        split = jnp.where(column < cells, high, mat - high).astype(bf16)
        vh = values.astype(bf16)
        vl = (values - vh.astype(f32)).astype(bf16)
        return jnp.dot(
            jnp.concatenate([split, split], axis=1),
            jnp.concatenate([vh, vh, vl, vl], axis=0),
            preferred_element_type=f32,
        )

    def outgoing(ps, f, x, result):
        edge = isinstance(x, int)
        for kind in range(2):
            for way in range(2):
                at = cells + 8 * way + kind
                row = result[at : at + 1]
                if edge:
                    es[ps, f, int(x > 0), way, kind : kind + 1, :] = row
                else:
                    zs[ps, way, f, kind, pl.ds(x, 1), :] = row

    def inner(f, x):
        result = product(0, f, x, gv[f, x + 1])
        outgoing(0, f, x, result)
        gv[f, x + 1] = result[:cells]

    def outer(f, x):
        own = gv[f, x + 1]
        smooth = own - smooth_weight * (gv[f, x + 2] - 2.0 * own + gv[f, x])
        result = product(1, f, x, smooth)
        outgoing(1, f, x, result)
        o_ref[f, x] = result[:cells]

    def finish(ps, f, x, halo=None):
        ref, line = (gv, x + 1) if ps == 0 else (o_ref, x)
        if halo is not None:
            line = halo * (lines + 1)
        log_ratio, amp, delta = line_values(f, x)
        if ps == 0:
            from_left = amp * etab[1] * jnp.exp(etab[0] * log_ratio)
            from_right = amp * etab[3] * jnp.exp(etab[2] * log_ratio)
            if halo is None:
                weights[f, x, 0] = from_left
                weights[f, x, 1] = from_right
        else:
            from_left, from_right = weights[f, x, 0], weights[f, x, 1]
        ie8 = lax.broadcasted_iota(jnp.int32, (8, LANES), 0)
        first8 = jnp.where(ie8 == 0, delta, 0.0)
        last8 = jnp.where(ie8 == 7, -delta, 0.0)
        if isinstance(x, int):
            rows = er.at[ps, f, int(x > 0)] if halo is None else hx.at[f, halo]
            low, high, low1, high1 = (
                rows[way, kind : kind + 1, :] for kind in range(2) for way in range(2)
            )
        else:
            low, high, low1, high1 = (
                zr[ps, way, f, kind, pl.ds(x, 1), :] for kind in range(2) for way in range(2)
            )
        for c in range(0, width, LANES):
            cols = slice(c, c + LANES)
            value = ref[f, line, :, cols] + from_left * low[:, cols] + from_right * high[:, cols]
            head = value[:8] + first8 * low1[:, cols]
            tail = value[cells - 8 :] + last8 * high1[:, cols]
            ref[f, line, :, cols] = jnp.concatenate([head, value[8 : cells - 8], tail], axis=0)

    def loop(low, high, body, unroll=1):
        def step(x, _):
            body(x)
            return 0

        lax.fori_loop(low, high, step, 0, unroll=unroll)

    def both(copy, ps, f, act):
        for way in range(2):
            getattr(copy(ps, way, f), act)()

    for copy in edges:
        copy.wait()

    def edges_in(f):
        inner(f, 0)
        inner(f, last)
        both(e_copy, 0, f, "start")

    def inside_in(f):
        load(f).wait()
        loop(1, last, lambda x: inner(f, x), last - 1)
        both(z_copy, 0, f, "start")

    def edges_first(f):
        both(e_copy, 0, f, "wait_recv")
        finish(0, f, 0)
        finish(0, f, last)

        @pl.when(f >= early)
        def _():
            send_lines(f)

        @pl.when(f < early)
        def _():
            for way, there in enumerate((has_low, has_high)):
                @pl.when(there)
                def _():
                    row_copy(way, f).start()

    def inside_first(f):
        both(z_copy, 0, f, "wait_recv")
        loop(1, last, lambda x: finish(0, f, x), last - 1)

    def inside_out(f):
        loop(1, last, lambda x: outer(f, x), last - 1)
        both(z_copy, 1, f, "start")

    def inside_last(f):
        both(z_copy, 1, f, "wait_recv")
        loop(1, last, lambda x: finish(1, f, x), last - 1)

    def relays_at(phase):
        for f in range(fields):
            if min(f, 4) == phase:
                relay(f)

    loop(0, fields, edges_in)
    inside_in(0)
    loop(0, fields, edges_first)
    relays_at(0)
    loop(1, fields, inside_in)
    relays_at(1)
    loop(0, fields, inside_first)
    relays_at(2)
    loop(0, fields, inside_out)
    relays_at(3)
    loop(0, fields, inside_last)
    relays_at(4)

    def halo_ready(side):
        for copy in neighbour_copies(1 - side):
            copy.wait_recv()
        line, row = (last, lines) if side == 0 else (0, lines + 1)
        for k, values in enumerate(line_coefs(alpha_n[side])):
            for f in range(early):
                coef[k, f, row : row + 1] = jnp.broadcast_to(values[f : f + 1, line : line + 1], (1, LANES))
        values = metric_n[side, line : line + 1, :]
        metrics[0, row : row + 1] = jnp.concatenate([values, values], axis=1)

    def halo_first(f, side):
        row_copy(1 - side, f).wait_recv()
        line = side * (lines + 1)
        gv[f, line] = product(0, f, lines + side, gv[f, line], False)[:cells]
        finish(0, f, lines + side, side)

    for side, there in enumerate((has_low, has_high)):
        @pl.when(there)
        def _():
            halo_ready(side)

    def edges_last(t):
        @pl.when(t < fields)
        def _():
            wait_lines(t)

            @pl.when(t < early)
            def _():
                for side, there in enumerate((has_low, has_high)):
                    @pl.when(there)
                    def _():
                        halo_first(t, side)

            outer(t, 0)
            outer(t, last)
            both(e_copy, 1, t, "start")

        @pl.when(t >= 1)
        def _():
            f = t - 1
            both(e_copy, 1, f, "wait_recv")
            finish(1, f, 0)
            finish(1, f, last)

    loop(0, fields + 1, edges_last)

    def drain(f):
        for ps in range(2):
            both(z_copy, ps, f, "wait_send")
            both(e_copy, ps, f, "wait_send")
        lines_sent(f)

    loop(0, fields, drain)
    for way, there in enumerate((has_low, has_high)):
        @pl.when(there)
        def _():
            for copy in neighbour_copies(way):
                copy.wait_send()
            for f in range(early):
                row_copy(way, f).wait_send()


def body(bricks, peers, grad_field, alpha_coef, metric_inner, metric_outer):
    fields, lines, cells, width = grad_field.shape
    dma = pltpu.SemaphoreType.DMA
    early = min(2, fields)
    far = pl.BlockSpec(memory_space=pltpu.HBM)
    return pl.pallas_call(
        functools.partial(kernel, bricks, peers, early),
        out_shape=jax.ShapeDtypeStruct(grad_field.shape, f32),
        in_specs=[far] * 4,
        out_specs=pl.BlockSpec(memory_space=pltpu.VMEM),
        scratch_shapes=[
            pltpu.VMEM((fields, lines + 2, cells, width), f32),
            pltpu.VMEM((fields, lines), f32),
            pltpu.VMEM((2, lines, cells), f32),
            pltpu.VMEM((2, fields, lines), f32),
            pltpu.VMEM((2, lines, cells), f32),
            pltpu.VMEM((2, lines + 8, 2 * cells), f32),
            pltpu.VMEM((3, fields, lines + 8, LANES), f32),
            pltpu.VMEM((fields, cells, width), f32),
            pltpu.VMEM((2, 2, fields, 2, lines, width), f32),
            pltpu.VMEM((2, 2, fields, 2, lines, width), f32),
            pltpu.VMEM((2, fields, 2, 2, 2, width), f32),
            pltpu.VMEM((2, fields, 2, 2, 2, width), f32),
            pltpu.VMEM((early, 2, 2, 2, width), f32),
            pltpu.VMEM((4, cells + 16, 2 * cells), f32),
            pltpu.VMEM((4, cells, LANES), f32),
            pltpu.VMEM((fields, lines, cells + 16, 2 * cells), f32),
            pltpu.VMEM((fields, lines, 2, cells, LANES), f32),
            dma((2, 2)), dma((2, 2)), dma((2, early)), dma((2, early)),
            dma((3,)), dma((2,)), dma((fields,)),
            dma((2, 2, fields)), dma((2, 2, fields)), dma((2, 2, fields)), dma((2, 2, fields)),
            dma((2, fields)), dma((2, fields)), dma((fields,)), dma((fields,)),
        ],
        compiler_params=pltpu.CompilerParams(
            collective_id=0, has_side_effects=True, vmem_limit_bytes=40 * 1024 * 1024
        ),
    )(*(pltpu.with_memory_space_constraint(a, pltpu.HBM) for a in (grad_field, alpha_coef, metric_inner, metric_outer)))


def solution(mesh):
    placed = (P(None, "brick", "gz", None), P(None, "brick"), P("brick", "gz"), P("brick", "gz"))
    return jax.shard_map(
        functools.partial(body, mesh.shape["brick"], mesh.shape["gz"]),
        mesh=mesh, in_specs=placed, out_specs=P(None, "brick", "gz", None), check_vma=False,
    )
```

```python
import functools

import jax
import jax.numpy as jnp
from jax import lax
from jax.experimental import pallas as pl
from jax.experimental.pallas import tpu as pltpu
from jax.sharding import PartitionSpec as P

smooth_weight = 0.2
MESH = pl.DeviceIdType.MESH
f32, bf16 = jnp.float32, jnp.bfloat16
LANES = 128


def line_coefs(alpha):
    ratio = 2.0 * alpha / (1.0 + jnp.sqrt(1.0 - 4.0 * alpha * alpha))
    scale = (ratio / alpha) / (1.0 - ratio * ratio)
    near = 2.0 * (alpha + 2.0) / 3.0
    far = (4.0 * alpha - 1.0) / 3.0
    p, q = -ratio, -1.0 / ratio
    amp = -scale * (near * 0.5 * (p - q) + far * 0.25 * (p * p - q * q))
    delta = scale * far * 0.25 * (p - q)
    return jnp.log(ratio), amp, delta


def parity(n):
    return 1.0 - 2.0 * lax.rem(n, 2).astype(f32)


def kernel(
    bricks, peers, early, g_ref, alpha_ref, metric_in_ref, metric_out_ref, o_ref,
    gv, alpha_v, metric_v, alpha_n, metric_n, metrics, coef, rb, zs, zr, es, er, hx, tab, etab, mats, weights,
    ns_sem, nr_sem, hs_sem, hr_sem, small_sem, edge_sem, load_sem, zs_sem, zr_sem, es_sem, er_sem, xs_sem, xr_sem, rs_sem, rr_sem,
):
    fields, lines, cells, width = o_ref.shape
    b, d = lax.axis_index("brick"), lax.axis_index("gz")
    right, left = lax.rem(d + 1, peers), lax.rem(d + peers - 1, peers)
    has_low, has_high = b > 0, b < bricks - 1
    odd, core = lax.rem(b, 2), lax.rem(d, 2)
    paired = bricks % 2 == 0
    toward = 1 - 2 * odd
    last = lines - 1

    def local(src, dst, sem):
        return pltpu.make_async_copy(src, dst, sem)

    small = [
        local(alpha_ref, alpha_v, small_sem.at[0]),
        local(metric_in_ref, metric_v.at[0], small_sem.at[1]),
        local(metric_out_ref, metric_v.at[1], small_sem.at[2]),
    ]
    edges = [local(g_ref.at[:, x], gv.at[:, x + 1], edge_sem.at[k]) for k, x in enumerate((0, last))]

    def load(f):
        return local(g_ref.at[f, pl.ds(1, lines - 2)], gv.at[f, pl.ds(2, lines - 2)], load_sem.at[f])

    def remote(src, dst, send_sem, recv_sem, to):
        return pltpu.make_async_remote_copy(
            src_ref=src, dst_ref=dst, send_sem=send_sem, recv_sem=recv_sem,
            device_id=to, device_id_type=MESH,
        )

    def z_copy(ps, way, f):
        to = {"gz": right if way == 0 else left}
        return remote(zs.at[ps, way, f], zr.at[ps, way, f], zs_sem.at[ps, way, f], zr_sem.at[ps, way, f], to)

    def e_copy(ps, way, f):
        to = {"gz": right if way == 0 else left}
        return remote(es.at[ps, f, :, way], er.at[ps, f, :, way], es_sem.at[ps, way, f], er_sem.at[ps, way, f], to)

    def x_copy(way, f, raw=False):
        src, dst, to = (0, lines + 1, b - 1) if way == 0 else (last, 0, b + 1)
        return remote(line_of(f, src, raw), gv.at[f, dst], xs_sem.at[way, f], xr_sem.at[way, f], {"brick": to})

    def line_of(f, index, raw):
        return g_ref.at[f, index] if raw else gv.at[f, index + 1]

    def pair_copy(f, raw=False):
        src = line_of(f, jnp.where(odd == 1, 0, last), raw)
        dst = jnp.where(odd == 1, lines + 1, 0)
        return remote(
            src, gv.at[f, dst], xs_sem.at[0, f], xr_sem.at[1 - odd, f], {"brick": b + toward}
        )

    def far_line(f, raw):
        return line_of(f, jnp.where(odd == 1, last, 0), raw)

    def straight_copy(f, raw=False):
        dst = jnp.where(odd == 1, 0, lines + 1)
        return remote(
            far_line(f, raw), gv.at[f, dst], xs_sem.at[1, f], xr_sem.at[odd, f], {"brick": b - toward}
        )

    def hop_copy(f, raw=False):
        return remote(far_line(f, raw), rb.at[f], xs_sem.at[1, f], rr_sem.at[f], {"brick": b - 2 * toward})

    def relay_copy(f):
        dst = jnp.where(odd == 1, 0, lines + 1)
        return remote(rb.at[f], gv.at[f, dst], rs_sem.at[f], xr_sem.at[odd, f], {"brick": b + toward})

    far = ((odd == 1) & has_high) | ((odd == 0) & has_low)
    straight, hops = far & (core == 0), far & (core == 1)
    relays = (b + 2 * toward >= 0) & (b + 2 * toward < bricks) & (core == 1)

    def send_lines(f, raw=False):
        if paired:
            @pl.when(hops)
            def _():
                hop_copy(f, raw).start()

            @pl.when(straight)
            def _():
                straight_copy(f, raw).start()

            pair_copy(f, raw).start()
        else:
            @pl.when(has_low)
            def _():
                x_copy(0, f, raw).start()

            @pl.when(has_high)
            def _():
                x_copy(1, f, raw).start()

    def beside(way):
        return {"brick": b - 1 if way == 0 else b + 1}

    def neighbour_copies(way):
        return [
            remote(src, dst.at[1 - way], ns_sem.at[way, k], nr_sem.at[way, k], beside(way))
            for k, (src, dst) in enumerate(((alpha_ref, alpha_n), (metric_in_ref, metric_n)))
        ]

    def row_copy(way, f):
        return remote(er.at[0, f, way], hx.at[f, 1 - way], hs_sem.at[way, f], hr_sem.at[way, f], beside(way))

    def relay(f):
        if paired:
            @pl.when(relays)
            def _():
                hop_copy(f).wait_recv()
                relay_copy(f).start()

    def wait_lines(f):
        @pl.when(has_high)
        def _():
            x_copy(0, f).wait_recv()

        @pl.when(has_low)
        def _():
            x_copy(1, f).wait_recv()

    def lines_sent(f):
        if paired:
            pair_copy(f).wait_send()

            @pl.when(far)
            def _():
                hop_copy(f).wait_send()

            @pl.when(relays)
            def _():
                relay_copy(f).wait_send()
        else:
            @pl.when(has_low)
            def _():
                x_copy(0, f).wait_send()

            @pl.when(has_high)
            def _():
                x_copy(1, f).wait_send()

    barrier = pltpu.get_barrier_semaphore()
    for z in (left, right):
        pl.semaphore_signal(barrier, inc=1, device_id={"gz": z}, device_id_type=MESH)
    expected = 2
    for step in (-2, -1, 1, 2):
        there = (b + step >= 0) & (b + step < bricks)
        expected = expected + jnp.where(there, 1, 0)

        @pl.when(there)
        def _():
            pl.semaphore_signal(barrier, inc=1, device_id={"brick": b + step}, device_id_type=MESH)

    for copy in small + edges:
        copy.start()
    for f in range(fields):
        load(f).start()

    pl.semaphore_wait(barrier, expected)
    for f in range(early):
        send_lines(f, True)
    for way, there in enumerate((has_low, has_high)):
        @pl.when(there)
        def _():
            for copy in neighbour_copies(way):
                copy.start()

    rows = cells + 16
    i = lax.broadcasted_iota(jnp.int32, (rows, 2 * cells), 0)
    j = lax.rem(lax.broadcasted_iota(jnp.int32, (rows, 2 * cells), 1), cells)
    n = i - j
    main = i < cells
    to_right, to_left = i == cells, i == cells + 8
    dist = jnp.where(main, jnp.abs(n), jnp.where(to_right, cells - 1 - j, j))
    side = jnp.where(n > 0, 1.0, jnp.where(n < 0, -1.0, 0.0))
    tab[0] = dist.astype(f32)
    tab[1] = jnp.where(main, side, jnp.where(to_right | to_left, 1.0, 0.0)) * parity(dist)
    tab[2] = jnp.where(main & (dist == 1), side, 0.0)
    pick = ((i == cells + 1) & (j == cells - 1)) | ((i == cells + 9) & (j == 0))
    tab[3] = jnp.where(pick, 1.0, 0.0)
    ie = lax.broadcasted_iota(jnp.int32, (cells, LANES), 0)
    etab[0] = (ie + 1).astype(f32)
    etab[1] = parity(ie + 1)
    etab[2] = (cells - ie).astype(f32)
    etab[3] = -parity(cells - ie)

    @pl.when(jnp.logical_not(has_low))
    def _():
        gv[:, 0] = jnp.zeros((fields, cells, width), f32)

    @pl.when(jnp.logical_not(has_high))
    def _():
        gv[:, lines + 1] = jnp.zeros((fields, cells, width), f32)

    for copy in small:
        copy.wait()
    diagonal = lax.broadcasted_iota(jnp.int32, (lines, lines), 0) == lax.broadcasted_iota(
        jnp.int32, (lines, lines), 1
    )
    for k, values in enumerate(line_coefs(alpha_v[...])):
        for f in range(fields):
            column = jnp.sum(jnp.where(diagonal, values[f : f + 1], 0.0), axis=1, keepdims=True)
            coef[k, f, :lines] = jnp.broadcast_to(column, (lines, LANES))
    for k in range(2):
        metrics[k, :lines] = jnp.concatenate([metric_v[k], metric_v[k]], axis=1)

    def line_values(f, x):
        return (coef[k, f, pl.ds(x, 1), :] for k in range(3))

    def product(ps, f, x, values, keep=True):
        if ps == 0:
            log_ratio, amp, delta = line_values(f, x)
            powers = tab[1] * jnp.exp(tab[0] * log_ratio)
            mat = jnp.concatenate([powers[:cells] * amp, powers[cells:]], axis=0)
            mat = mat + tab[2] * delta + tab[3]
            if keep:
                mats[f, x] = mat
        else:
            mat = mats[f, x]
        mat = mat * metrics[ps, pl.ds(x, 1), :]
        high = mat.astype(bf16).astype(f32)
        column = lax.broadcasted_iota(jnp.int32, mat.shape, 1)
        split = jnp.where(column < cells, high, mat - high).astype(bf16)
        vh = values.astype(bf16)
        vl = (values - vh.astype(f32)).astype(bf16)
        return jnp.dot(
            jnp.concatenate([split, split], axis=1),
            jnp.concatenate([vh, vh, vl, vl], axis=0),
            preferred_element_type=f32,
        )

    def outgoing(ps, f, x, result):
        edge = isinstance(x, int)
        for kind in range(2):
            for way in range(2):
                at = cells + 8 * way + kind
                row = result[at : at + 1]
                if edge:
                    es[ps, f, int(x > 0), way, kind : kind + 1, :] = row
                else:
                    zs[ps, way, f, kind, pl.ds(x, 1), :] = row

    def inner(f, x):
        result = product(0, f, x, gv[f, x + 1])
        outgoing(0, f, x, result)
        gv[f, x + 1] = result[:cells]

    def outer(f, x):
        own = gv[f, x + 1]
        smooth = own - smooth_weight * (gv[f, x + 2] - 2.0 * own + gv[f, x])
        result = product(1, f, x, smooth)
        outgoing(1, f, x, result)
        o_ref[f, x] = result[:cells]

    def finish(ps, f, x, halo=None):
        ref, line = (gv, x + 1) if ps == 0 else (o_ref, x)
        if halo is not None:
            line = halo * (lines + 1)
        log_ratio, amp, delta = line_values(f, x)
        if ps == 0:
            from_left = amp * etab[1] * jnp.exp(etab[0] * log_ratio)
            from_right = amp * etab[3] * jnp.exp(etab[2] * log_ratio)
            if halo is None:
                weights[f, x, 0] = from_left
                weights[f, x, 1] = from_right
        else:
            from_left, from_right = weights[f, x, 0], weights[f, x, 1]
        ie8 = lax.broadcasted_iota(jnp.int32, (8, LANES), 0)
        first8 = jnp.where(ie8 == 0, delta, 0.0)
        last8 = jnp.where(ie8 == 7, -delta, 0.0)
        if isinstance(x, int):
            rows = er.at[ps, f, int(x > 0)] if halo is None else hx.at[f, halo]
            low, high, low1, high1 = (
                rows[way, kind : kind + 1, :] for kind in range(2) for way in range(2)
            )
        else:
            low, high, low1, high1 = (
                zr[ps, way, f, kind, pl.ds(x, 1), :] for kind in range(2) for way in range(2)
            )
        for c in range(0, width, LANES):
            cols = slice(c, c + LANES)
            value = ref[f, line, :, cols] + from_left * low[:, cols] + from_right * high[:, cols]
            head = value[:8] + first8 * low1[:, cols]
            tail = value[cells - 8 :] + last8 * high1[:, cols]
            ref[f, line, :, cols] = jnp.concatenate([head, value[8 : cells - 8], tail], axis=0)

    def loop(low, high, body, unroll=1):
        def step(x, _):
            body(x)
            return 0

        lax.fori_loop(low, high, step, 0, unroll=unroll)

    def both(copy, ps, f, act):
        for way in range(2):
            getattr(copy(ps, way, f), act)()

    for copy in edges:
        copy.wait()

    def edges_in(f):
        inner(f, 0)
        inner(f, last)
        both(e_copy, 0, f, "start")

    def inside_in(f):
        load(f).wait()
        loop(1, last, lambda x: inner(f, x), last - 1)
        both(z_copy, 0, f, "start")

    def edges_first(f):
        both(e_copy, 0, f, "wait_recv")
        finish(0, f, 0)
        finish(0, f, last)

        @pl.when(f >= early)
        def _():
            send_lines(f)

        @pl.when(f < early)
        def _():
            for way, there in enumerate((has_low, has_high)):
                @pl.when(there)
                def _():
                    row_copy(way, f).start()

    def inside_first(f):
        both(z_copy, 0, f, "wait_recv")
        loop(1, last, lambda x: finish(0, f, x), last - 1)

    def inside_out(f):
        loop(1, last, lambda x: outer(f, x), last - 1)
        both(z_copy, 1, f, "start")

    def inside_last(f):
        both(z_copy, 1, f, "wait_recv")
        loop(1, last, lambda x: finish(1, f, x), last - 1)

    loop(0, fields, edges_in)
    inside_in(0)
    loop(0, fields, edges_first)
    loop(0, early, relay)
    loop(1, fields, inside_in)
    loop(early, fields, relay)
    loop(0, fields, inside_first)
    loop(0, fields, inside_out)
    loop(0, fields, inside_last)

    def halo_ready(side):
        for copy in neighbour_copies(1 - side):
            copy.wait_recv()
        line, row = (last, lines) if side == 0 else (0, lines + 1)
        for k, values in enumerate(line_coefs(alpha_n[side])):
            for f in range(early):
                coef[k, f, row : row + 1] = jnp.broadcast_to(values[f : f + 1, line : line + 1], (1, LANES))
        values = metric_n[side, line : line + 1, :]
        metrics[0, row : row + 1] = jnp.concatenate([values, values], axis=1)

    def halo_first(f, side):
        row_copy(1 - side, f).wait_recv()
        line = side * (lines + 1)
        gv[f, line] = product(0, f, lines + side, gv[f, line], False)[:cells]
        finish(0, f, lines + side, side)

    for side, there in enumerate((has_low, has_high)):
        @pl.when(there)
        def _():
            halo_ready(side)

    def edges_last(t):
        @pl.when(t < fields)
        def _():
            wait_lines(t)

            @pl.when(t < early)
            def _():
                for side, there in enumerate((has_low, has_high)):
                    @pl.when(there)
                    def _():
                        halo_first(t, side)

            outer(t, 0)
            outer(t, last)
            both(e_copy, 1, t, "start")

        @pl.when(t >= 1)
        def _():
            f = t - 1
            both(e_copy, 1, f, "wait_recv")
            finish(1, f, 0)
            finish(1, f, last)

    loop(0, fields + 1, edges_last)

    def drain(f):
        for ps in range(2):
            both(z_copy, ps, f, "wait_send")
            both(e_copy, ps, f, "wait_send")
        lines_sent(f)

    loop(0, fields, drain)
    for way, there in enumerate((has_low, has_high)):
        @pl.when(there)
        def _():
            for copy in neighbour_copies(way):
                copy.wait_send()
            for f in range(early):
                row_copy(way, f).wait_send()


def body(bricks, peers, grad_field, alpha_coef, metric_inner, metric_outer):
    fields, lines, cells, width = grad_field.shape
    dma = pltpu.SemaphoreType.DMA
    early = min(2, fields)
    far = pl.BlockSpec(memory_space=pltpu.HBM)
    return pl.pallas_call(
        functools.partial(kernel, bricks, peers, early),
        out_shape=jax.ShapeDtypeStruct(grad_field.shape, f32),
        in_specs=[far] * 4,
        out_specs=pl.BlockSpec(memory_space=pltpu.VMEM),
        scratch_shapes=[
            pltpu.VMEM((fields, lines + 2, cells, width), f32),
            pltpu.VMEM((fields, lines), f32),
            pltpu.VMEM((2, lines, cells), f32),
            pltpu.VMEM((2, fields, lines), f32),
            pltpu.VMEM((2, lines, cells), f32),
            pltpu.VMEM((2, lines + 8, 2 * cells), f32),
            pltpu.VMEM((3, fields, lines + 8, LANES), f32),
            pltpu.VMEM((fields, cells, width), f32),
            pltpu.VMEM((2, 2, fields, 2, lines, width), f32),
            pltpu.VMEM((2, 2, fields, 2, lines, width), f32),
            pltpu.VMEM((2, fields, 2, 2, 2, width), f32),
            pltpu.VMEM((2, fields, 2, 2, 2, width), f32),
            pltpu.VMEM((early, 2, 2, 2, width), f32),
            pltpu.VMEM((4, cells + 16, 2 * cells), f32),
            pltpu.VMEM((4, cells, LANES), f32),
            pltpu.VMEM((fields, lines, cells + 16, 2 * cells), f32),
            pltpu.VMEM((fields, lines, 2, cells, LANES), f32),
            dma((2, 2)), dma((2, 2)), dma((2, early)), dma((2, early)),
            dma((3,)), dma((2,)), dma((fields,)),
            dma((2, 2, fields)), dma((2, 2, fields)), dma((2, 2, fields)), dma((2, 2, fields)),
            dma((2, fields)), dma((2, fields)), dma((fields,)), dma((fields,)),
        ],
        compiler_params=pltpu.CompilerParams(
            collective_id=0, has_side_effects=True, vmem_limit_bytes=40 * 1024 * 1024
        ),
    )(*(pltpu.with_memory_space_constraint(a, pltpu.HBM) for a in (grad_field, alpha_coef, metric_inner, metric_outer)))


def solution(mesh):
    placed = (P(None, "brick", "gz", None), P(None, "brick"), P("brick", "gz"), P("brick", "gz"))
    return jax.shard_map(
        functools.partial(body, mesh.shape["brick"], mesh.shape["gz"]),
        mesh=mesh, in_specs=placed, out_specs=P(None, "brick", "gz", None), check_vma=False,
    )
```

```python
import functools

import jax
import jax.numpy as jnp
from jax import lax
from jax.experimental import pallas as pl
from jax.experimental.pallas import tpu as pltpu
from jax.sharding import PartitionSpec as P

smooth_weight = 0.2
MESH = pl.DeviceIdType.MESH
f32, bf16 = jnp.float32, jnp.bfloat16
LANES = 128


def line_coefs(alpha):
    ratio = 2.0 * alpha / (1.0 + jnp.sqrt(1.0 - 4.0 * alpha * alpha))
    scale = (ratio / alpha) / (1.0 - ratio * ratio)
    near = 2.0 * (alpha + 2.0) / 3.0
    far = (4.0 * alpha - 1.0) / 3.0
    p, q = -ratio, -1.0 / ratio
    amp = -scale * (near * 0.5 * (p - q) + far * 0.25 * (p * p - q * q))
    delta = scale * far * 0.25 * (p - q)
    return jnp.log(ratio), amp, delta


def parity(n):
    return 1.0 - 2.0 * lax.rem(n, 2).astype(f32)


def kernel(
    bricks, peers, early, g_ref, alpha_ref, metric_in_ref, metric_out_ref, o_ref,
    gv, alpha_v, metric_v, alpha_n, metric_n, metrics, coef, rb, zs, zr, es, er, hx, tab, etab, mats, weights,
    ns_sem, nr_sem, hs_sem, hr_sem, small_sem, edge_sem, load_sem, zs_sem, zr_sem, es_sem, er_sem, xs_sem, xr_sem, rs_sem, rr_sem,
):
    fields, lines, cells, width = o_ref.shape
    b, d = lax.axis_index("brick"), lax.axis_index("gz")
    right, left = lax.rem(d + 1, peers), lax.rem(d + peers - 1, peers)
    has_low, has_high = b > 0, b < bricks - 1
    odd, core = lax.rem(b, 2), lax.rem(d, 2)
    paired = bricks % 2 == 0
    toward = 1 - 2 * odd
    last = lines - 1

    def local(src, dst, sem):
        return pltpu.make_async_copy(src, dst, sem)

    small = [
        local(alpha_ref, alpha_v, small_sem.at[0]),
        local(metric_in_ref, metric_v.at[0], small_sem.at[1]),
        local(metric_out_ref, metric_v.at[1], small_sem.at[2]),
    ]
    edges = [local(g_ref.at[:, x], gv.at[:, x + 1], edge_sem.at[k]) for k, x in enumerate((0, last))]

    def load(f):
        return local(g_ref.at[f, pl.ds(1, lines - 2)], gv.at[f, pl.ds(2, lines - 2)], load_sem.at[f])

    def remote(src, dst, send_sem, recv_sem, to):
        return pltpu.make_async_remote_copy(
            src_ref=src, dst_ref=dst, send_sem=send_sem, recv_sem=recv_sem,
            device_id=to, device_id_type=MESH,
        )

    def z_copy(ps, way, f):
        to = {"gz": right if way == 0 else left}
        return remote(zs.at[ps, way, f], zr.at[ps, way, f], zs_sem.at[ps, way, f], zr_sem.at[ps, way, f], to)

    def e_copy(ps, way, f):
        to = {"gz": right if way == 0 else left}
        return remote(es.at[ps, f, :, way], er.at[ps, f, :, way], es_sem.at[ps, way, f], er_sem.at[ps, way, f], to)

    def x_copy(way, f, raw=False):
        src, dst, to = (0, lines + 1, b - 1) if way == 0 else (last, 0, b + 1)
        return remote(line_of(f, src, raw), gv.at[f, dst], xs_sem.at[way, f], xr_sem.at[way, f], {"brick": to})

    def line_of(f, index, raw):
        return g_ref.at[f, index] if raw else gv.at[f, index + 1]

    def pair_copy(f, raw=False):
        src = line_of(f, jnp.where(odd == 1, 0, last), raw)
        dst = jnp.where(odd == 1, lines + 1, 0)
        return remote(
            src, gv.at[f, dst], xs_sem.at[0, f], xr_sem.at[1 - odd, f], {"brick": b + toward}
        )

    def far_line(f, raw):
        return line_of(f, jnp.where(odd == 1, last, 0), raw)

    def straight_copy(f, raw=False):
        dst = jnp.where(odd == 1, 0, lines + 1)
        return remote(
            far_line(f, raw), gv.at[f, dst], xs_sem.at[1, f], xr_sem.at[odd, f], {"brick": b - toward}
        )

    def hop_copy(f, raw=False):
        return remote(far_line(f, raw), rb.at[f], xs_sem.at[1, f], rr_sem.at[f], {"brick": b - 2 * toward})

    def relay_copy(f):
        dst = jnp.where(odd == 1, 0, lines + 1)
        return remote(rb.at[f], gv.at[f, dst], rs_sem.at[f], xr_sem.at[odd, f], {"brick": b + toward})

    far = ((odd == 1) & has_high) | ((odd == 0) & has_low)
    straight, hops = far & (core == 0), far & (core == 1)
    relays = (b + 2 * toward >= 0) & (b + 2 * toward < bricks) & (core == 1)

    def send_lines(f, raw=False):
        if paired:
            @pl.when(hops)
            def _():
                hop_copy(f, raw).start()

            @pl.when(straight)
            def _():
                straight_copy(f, raw).start()

            pair_copy(f, raw).start()
        else:
            @pl.when(has_low)
            def _():
                x_copy(0, f, raw).start()

            @pl.when(has_high)
            def _():
                x_copy(1, f, raw).start()

    def beside(way):
        return {"brick": b - 1 if way == 0 else b + 1}

    def neighbour_copies(way):
        return [
            remote(src, dst.at[1 - way], ns_sem.at[way, k], nr_sem.at[way, k], beside(way))
            for k, (src, dst) in enumerate(((alpha_ref, alpha_n), (metric_in_ref, metric_n)))
        ]

    def row_copy(way, f):
        return remote(er.at[0, f, way], hx.at[f, 1 - way], hs_sem.at[way, f], hr_sem.at[way, f], beside(way))

    def relay(f):
        if paired:
            @pl.when(relays)
            def _():
                hop_copy(f).wait_recv()
                relay_copy(f).start()

    def wait_lines(f):
        @pl.when(has_high)
        def _():
            x_copy(0, f).wait_recv()

        @pl.when(has_low)
        def _():
            x_copy(1, f).wait_recv()

    def lines_sent(f):
        if paired:
            pair_copy(f).wait_send()

            @pl.when(far)
            def _():
                hop_copy(f).wait_send()

            @pl.when(relays)
            def _():
                relay_copy(f).wait_send()
        else:
            @pl.when(has_low)
            def _():
                x_copy(0, f).wait_send()

            @pl.when(has_high)
            def _():
                x_copy(1, f).wait_send()

    barrier = pltpu.get_barrier_semaphore()
    for z in (left, right):
        pl.semaphore_signal(barrier, inc=1, device_id={"gz": z}, device_id_type=MESH)
    expected = 2
    for step in (-2, -1, 1, 2):
        there = (b + step >= 0) & (b + step < bricks)
        expected = expected + jnp.where(there, 1, 0)

        @pl.when(there)
        def _():
            pl.semaphore_signal(barrier, inc=1, device_id={"brick": b + step}, device_id_type=MESH)

    for copy in small + edges:
        copy.start()
    for f in range(fields):
        load(f).start()

    pl.semaphore_wait(barrier, expected)
    for f in range(early):
        send_lines(f, True)
    for way, there in enumerate((has_low, has_high)):
        @pl.when(there)
        def _():
            for copy in neighbour_copies(way):
                copy.start()

    rows = cells + 16
    i = lax.broadcasted_iota(jnp.int32, (rows, 2 * cells), 0)
    j = lax.rem(lax.broadcasted_iota(jnp.int32, (rows, 2 * cells), 1), cells)
    n = i - j
    main = i < cells
    to_right, to_left = i == cells, i == cells + 8
    dist = jnp.where(main, jnp.abs(n), jnp.where(to_right, cells - 1 - j, j))
    side = jnp.where(n > 0, 1.0, jnp.where(n < 0, -1.0, 0.0))
    tab[0] = dist.astype(f32)
    tab[1] = jnp.where(main, side, jnp.where(to_right | to_left, 1.0, 0.0)) * parity(dist)
    tab[2] = jnp.where(main & (dist == 1), side, 0.0)
    pick = ((i == cells + 1) & (j == cells - 1)) | ((i == cells + 9) & (j == 0))
    tab[3] = jnp.where(pick, 1.0, 0.0)
    ie = lax.broadcasted_iota(jnp.int32, (cells, LANES), 0)
    etab[0] = (ie + 1).astype(f32)
    etab[1] = parity(ie + 1)
    etab[2] = (cells - ie).astype(f32)
    etab[3] = -parity(cells - ie)

    @pl.when(jnp.logical_not(has_low))
    def _():
        gv[:, 0] = jnp.zeros((fields, cells, width), f32)

    @pl.when(jnp.logical_not(has_high))
    def _():
        gv[:, lines + 1] = jnp.zeros((fields, cells, width), f32)

    for copy in small:
        copy.wait()
    diagonal = lax.broadcasted_iota(jnp.int32, (lines, lines), 0) == lax.broadcasted_iota(
        jnp.int32, (lines, lines), 1
    )
    for k, values in enumerate(line_coefs(alpha_v[...])):
        for f in range(fields):
            column = jnp.sum(jnp.where(diagonal, values[f : f + 1], 0.0), axis=1, keepdims=True)
            coef[k, f, :lines] = jnp.broadcast_to(column, (lines, LANES))
    for k in range(2):
        metrics[k, :lines] = jnp.concatenate([metric_v[k], metric_v[k]], axis=1)

    def line_values(f, x):
        return (coef[k, f, pl.ds(x, 1), :] for k in range(3))

    def product(ps, f, x, values, keep=True):
        if ps == 0:
            log_ratio, amp, delta = line_values(f, x)
            powers = tab[1] * jnp.exp(tab[0] * log_ratio)
            mat = jnp.concatenate([powers[:cells] * amp, powers[cells:]], axis=0)
            mat = mat + tab[2] * delta + tab[3]
            if keep:
                mats[f, x] = mat
        else:
            mat = mats[f, x]
        mat = mat * metrics[ps, pl.ds(x, 1), :]
        high = mat.astype(bf16).astype(f32)
        column = lax.broadcasted_iota(jnp.int32, mat.shape, 1)
        split = jnp.where(column < cells, high, mat - high).astype(bf16)
        vh = values.astype(bf16)
        vl = (values - vh.astype(f32)).astype(bf16)
        return jnp.dot(
            jnp.concatenate([split, split], axis=1),
            jnp.concatenate([vh, vh, vl, vl], axis=0),
            preferred_element_type=f32,
        )

    def outgoing(ps, f, x, result):
        edge = isinstance(x, int)
        for kind in range(2):
            for way in range(2):
                at = cells + 8 * way + kind
                row = result[at : at + 1]
                if edge:
                    es[ps, f, int(x > 0), way, kind : kind + 1, :] = row
                else:
                    zs[ps, way, f, kind, pl.ds(x, 1), :] = row

    def inner(f, x):
        result = product(0, f, x, gv[f, x + 1])
        outgoing(0, f, x, result)
        gv[f, x + 1] = result[:cells]

    def outer(f, x):
        own = gv[f, x + 1]
        smooth = own - smooth_weight * (gv[f, x + 2] - 2.0 * own + gv[f, x])
        result = product(1, f, x, smooth)
        outgoing(1, f, x, result)
        o_ref[f, x] = result[:cells]

    def finish(ps, f, x, halo=None):
        ref, line = (gv, x + 1) if ps == 0 else (o_ref, x)
        if halo is not None:
            line = halo * (lines + 1)
        log_ratio, amp, delta = line_values(f, x)
        if ps == 0:
            from_left = amp * etab[1] * jnp.exp(etab[0] * log_ratio)
            from_right = amp * etab[3] * jnp.exp(etab[2] * log_ratio)
            if halo is None:
                weights[f, x, 0] = from_left
                weights[f, x, 1] = from_right
        else:
            from_left, from_right = weights[f, x, 0], weights[f, x, 1]
        ie8 = lax.broadcasted_iota(jnp.int32, (8, LANES), 0)
        first8 = jnp.where(ie8 == 0, delta, 0.0)
        last8 = jnp.where(ie8 == 7, -delta, 0.0)
        if isinstance(x, int):
            rows = er.at[ps, f, int(x > 0)] if halo is None else hx.at[f, halo]
            low, high, low1, high1 = (
                rows[way, kind : kind + 1, :] for kind in range(2) for way in range(2)
            )
        else:
            low, high, low1, high1 = (
                zr[ps, way, f, kind, pl.ds(x, 1), :] for kind in range(2) for way in range(2)
            )
        for c in range(0, width, LANES):
            cols = slice(c, c + LANES)
            value = ref[f, line, :, cols] + from_left * low[:, cols] + from_right * high[:, cols]
            head = value[:8] + first8 * low1[:, cols]
            tail = value[cells - 8 :] + last8 * high1[:, cols]
            ref[f, line, :, cols] = jnp.concatenate([head, value[8 : cells - 8], tail], axis=0)

    def loop(low, high, body, unroll=1):
        def step(x, _):
            body(x)
            return 0

        lax.fori_loop(low, high, step, 0, unroll=unroll)

    def both(copy, ps, f, act):
        for way in range(2):
            getattr(copy(ps, way, f), act)()

    for copy in edges:
        copy.wait()

    def edges_in(f):
        inner(f, 0)
        inner(f, last)
        both(e_copy, 0, f, "start")

    def inside_in(f):
        load(f).wait()
        loop(1, last, lambda x: inner(f, x), last - 1)
        both(z_copy, 0, f, "start")

    def edges_first(f):
        both(e_copy, 0, f, "wait_recv")
        finish(0, f, 0)
        finish(0, f, last)

        @pl.when(f >= early)
        def _():
            send_lines(f)

        @pl.when(f < early)
        def _():
            for way, there in enumerate((has_low, has_high)):
                @pl.when(there)
                def _():
                    row_copy(way, f).start()

    def inside_first(f):
        both(z_copy, 0, f, "wait_recv")
        loop(1, last, lambda x: finish(0, f, x), last - 1)

    def inside_out(f):
        loop(1, last, lambda x: outer(f, x), last - 1)
        both(z_copy, 1, f, "start")

    def inside_last(f):
        both(z_copy, 1, f, "wait_recv")
        loop(1, last, lambda x: finish(1, f, x), last - 1)

    loop(0, fields, edges_in)
    inside_in(0)
    loop(0, fields, edges_first)
    loop(0, early, relay)
    loop(1, fields, inside_in)
    loop(early, fields, relay)
    loop(0, fields, inside_first)
    loop(0, fields, inside_out)
    loop(0, fields, inside_last)

    def halo_ready(side):
        for copy in neighbour_copies(1 - side):
            copy.wait_recv()
        line, row = (last, lines) if side == 0 else (0, lines + 1)
        for k, values in enumerate(line_coefs(alpha_n[side])):
            for f in range(early):
                coef[k, f, row : row + 1] = jnp.broadcast_to(values[f : f + 1, line : line + 1], (1, LANES))
        values = metric_n[side, line : line + 1, :]
        metrics[0, row : row + 1] = jnp.concatenate([values, values], axis=1)

    def halo_first(f, side):
        row_copy(1 - side, f).wait_recv()
        line = side * (lines + 1)
        gv[f, line] = product(0, f, lines + side, gv[f, line], False)[:cells]
        finish(0, f, lines + side, side)

    for side, there in enumerate((has_low, has_high)):
        @pl.when(there)
        def _():
            halo_ready(side)

    lag = 3

    def edges_last(t):
        @pl.when(t < fields)
        def _():
            wait_lines(t)

            @pl.when(t < early)
            def _():
                for side, there in enumerate((has_low, has_high)):
                    @pl.when(there)
                    def _():
                        halo_first(t, side)

            outer(t, 0)
            outer(t, last)
            both(e_copy, 1, t, "start")

        @pl.when(t >= lag)
        def _():
            f = t - lag
            both(e_copy, 1, f, "wait_recv")
            finish(1, f, 0)
            finish(1, f, last)

    loop(0, fields + lag, edges_last)

    def drain(f):
        for ps in range(2):
            both(z_copy, ps, f, "wait_send")
            both(e_copy, ps, f, "wait_send")
        lines_sent(f)

    loop(0, fields, drain)
    for way, there in enumerate((has_low, has_high)):
        @pl.when(there)
        def _():
            for copy in neighbour_copies(way):
                copy.wait_send()
            for f in range(early):
                row_copy(way, f).wait_send()


def body(bricks, peers, grad_field, alpha_coef, metric_inner, metric_outer):
    fields, lines, cells, width = grad_field.shape
    dma = pltpu.SemaphoreType.DMA
    early = min(2, fields)
    far = pl.BlockSpec(memory_space=pltpu.HBM)
    return pl.pallas_call(
        functools.partial(kernel, bricks, peers, early),
        out_shape=jax.ShapeDtypeStruct(grad_field.shape, f32),
        in_specs=[far] * 4,
        out_specs=pl.BlockSpec(memory_space=pltpu.VMEM),
        scratch_shapes=[
            pltpu.VMEM((fields, lines + 2, cells, width), f32),
            pltpu.VMEM((fields, lines), f32),
            pltpu.VMEM((2, lines, cells), f32),
            pltpu.VMEM((2, fields, lines), f32),
            pltpu.VMEM((2, lines, cells), f32),
            pltpu.VMEM((2, lines + 8, 2 * cells), f32),
            pltpu.VMEM((3, fields, lines + 8, LANES), f32),
            pltpu.VMEM((fields, cells, width), f32),
            pltpu.VMEM((2, 2, fields, 2, lines, width), f32),
            pltpu.VMEM((2, 2, fields, 2, lines, width), f32),
            pltpu.VMEM((2, fields, 2, 2, 2, width), f32),
            pltpu.VMEM((2, fields, 2, 2, 2, width), f32),
            pltpu.VMEM((early, 2, 2, 2, width), f32),
            pltpu.VMEM((4, cells + 16, 2 * cells), f32),
            pltpu.VMEM((4, cells, LANES), f32),
            pltpu.VMEM((fields, lines, cells + 16, 2 * cells), f32),
            pltpu.VMEM((fields, lines, 2, cells, LANES), f32),
            dma((2, 2)), dma((2, 2)), dma((2, early)), dma((2, early)),
            dma((3,)), dma((2,)), dma((fields,)),
            dma((2, 2, fields)), dma((2, 2, fields)), dma((2, 2, fields)), dma((2, 2, fields)),
            dma((2, fields)), dma((2, fields)), dma((fields,)), dma((fields,)),
        ],
        compiler_params=pltpu.CompilerParams(
            collective_id=0, has_side_effects=True, vmem_limit_bytes=40 * 1024 * 1024
        ),
    )(*(pltpu.with_memory_space_constraint(a, pltpu.HBM) for a in (grad_field, alpha_coef, metric_inner, metric_outer)))


def solution(mesh):
    placed = (P(None, "brick", "gz", None), P(None, "brick"), P("brick", "gz"), P("brick", "gz"))
    return jax.shard_map(
        functools.partial(body, mesh.shape["brick"], mesh.shape["gz"]),
        mesh=mesh, in_specs=placed, out_specs=P(None, "brick", "gz", None), check_vma=False,
    )
```

```python
import functools

import jax
import jax.numpy as jnp
from jax import lax
from jax.experimental import pallas as pl
from jax.experimental.pallas import tpu as pltpu
from jax.sharding import PartitionSpec as P

smooth_weight = 0.2
MESH = pl.DeviceIdType.MESH
f32, bf16 = jnp.float32, jnp.bfloat16
LANES = 128


def line_coefs(alpha):
    ratio = 2.0 * alpha / (1.0 + jnp.sqrt(1.0 - 4.0 * alpha * alpha))
    scale = (ratio / alpha) / (1.0 - ratio * ratio)
    near = 2.0 * (alpha + 2.0) / 3.0
    far = (4.0 * alpha - 1.0) / 3.0
    p, q = -ratio, -1.0 / ratio
    amp = -scale * (near * 0.5 * (p - q) + far * 0.25 * (p * p - q * q))
    delta = scale * far * 0.25 * (p - q)
    return jnp.log(ratio), amp, delta


def parity(n):
    return 1.0 - 2.0 * lax.rem(n, 2).astype(f32)


def kernel(
    bricks, peers, early, g_ref, alpha_ref, metric_in_ref, metric_out_ref, o_ref,
    gv, alpha_v, metric_v, alpha_n, metric_n, metrics, coef, rb, zs, zr, es, er, hx, tab, etab, mats, weights,
    ns_sem, nr_sem, hs_sem, hr_sem, small_sem, edge_sem, load_sem, zs_sem, zr_sem, es_sem, er_sem, xs_sem, xr_sem, rs_sem, rr_sem,
):
    fields, lines, cells, width = o_ref.shape
    b, d = lax.axis_index("brick"), lax.axis_index("gz")
    right, left = lax.rem(d + 1, peers), lax.rem(d + peers - 1, peers)
    has_low, has_high = b > 0, b < bricks - 1
    odd, core = lax.rem(b, 2), lax.rem(d, 2)
    paired = bricks % 2 == 0
    toward = 1 - 2 * odd
    last = lines - 1

    def local(src, dst, sem):
        return pltpu.make_async_copy(src, dst, sem)

    small = [
        local(alpha_ref, alpha_v, small_sem.at[0]),
        local(metric_in_ref, metric_v.at[0], small_sem.at[1]),
        local(metric_out_ref, metric_v.at[1], small_sem.at[2]),
    ]
    edges = [local(g_ref.at[:, x], gv.at[:, x + 1], edge_sem.at[k]) for k, x in enumerate((0, last))]

    def load(f):
        return local(g_ref.at[f, pl.ds(1, lines - 2)], gv.at[f, pl.ds(2, lines - 2)], load_sem.at[f])

    def remote(src, dst, send_sem, recv_sem, to):
        return pltpu.make_async_remote_copy(
            src_ref=src, dst_ref=dst, send_sem=send_sem, recv_sem=recv_sem,
            device_id=to, device_id_type=MESH,
        )

    def z_copy(ps, way, f):
        to = {"gz": right if way == 0 else left}
        return remote(zs.at[ps, way, f], zr.at[ps, way, f], zs_sem.at[ps, way, f], zr_sem.at[ps, way, f], to)

    def e_copy(ps, way, f):
        to = {"gz": right if way == 0 else left}
        return remote(es.at[ps, f, :, way], er.at[ps, f, :, way], es_sem.at[ps, way, f], er_sem.at[ps, way, f], to)

    def x_copy(way, f, raw=False):
        src, dst, to = (0, lines + 1, b - 1) if way == 0 else (last, 0, b + 1)
        return remote(line_of(f, src, raw), gv.at[f, dst], xs_sem.at[way, f], xr_sem.at[way, f], {"brick": to})

    def line_of(f, index, raw):
        return g_ref.at[f, index] if raw else gv.at[f, index + 1]

    def pair_copy(f, raw=False):
        src = line_of(f, jnp.where(odd == 1, 0, last), raw)
        dst = jnp.where(odd == 1, lines + 1, 0)
        return remote(
            src, gv.at[f, dst], xs_sem.at[0, f], xr_sem.at[1 - odd, f], {"brick": b + toward}
        )

    def far_line(f, raw):
        return line_of(f, jnp.where(odd == 1, last, 0), raw)

    def straight_copy(f, raw=False):
        dst = jnp.where(odd == 1, 0, lines + 1)
        return remote(
            far_line(f, raw), gv.at[f, dst], xs_sem.at[1, f], xr_sem.at[odd, f], {"brick": b - toward}
        )

    def hop_copy(f, raw=False):
        return remote(far_line(f, raw), rb.at[f], xs_sem.at[1, f], rr_sem.at[f], {"brick": b - 2 * toward})

    def relay_copy(f):
        dst = jnp.where(odd == 1, 0, lines + 1)
        return remote(rb.at[f], gv.at[f, dst], rs_sem.at[f], xr_sem.at[odd, f], {"brick": b + toward})

    far = ((odd == 1) & has_high) | ((odd == 0) & has_low)
    straight, hops = far & (core == 0), far & (core == 1)
    relays = (b + 2 * toward >= 0) & (b + 2 * toward < bricks) & (core == 1)

    def send_lines(f, raw=False):
        if paired:
            @pl.when(hops)
            def _():
                hop_copy(f, raw).start()

            @pl.when(straight)
            def _():
                straight_copy(f, raw).start()

            pair_copy(f, raw).start()
        else:
            @pl.when(has_low)
            def _():
                x_copy(0, f, raw).start()

            @pl.when(has_high)
            def _():
                x_copy(1, f, raw).start()

    def beside(way):
        return {"brick": b - 1 if way == 0 else b + 1}

    def neighbour_copies(way):
        return [
            remote(src, dst.at[1 - way], ns_sem.at[way, k], nr_sem.at[way, k], beside(way))
            for k, (src, dst) in enumerate(((alpha_ref, alpha_n), (metric_in_ref, metric_n)))
        ]

    def row_copy(way, f):
        return remote(er.at[0, f, way], hx.at[f, 1 - way], hs_sem.at[way, f], hr_sem.at[way, f], beside(way))

    def relay(f):
        if paired:
            @pl.when(relays)
            def _():
                hop_copy(f).wait_recv()
                relay_copy(f).start()

    def wait_lines(f):
        @pl.when(has_high)
        def _():
            x_copy(0, f).wait_recv()

        @pl.when(has_low)
        def _():
            x_copy(1, f).wait_recv()

    def lines_sent(f):
        if paired:
            pair_copy(f).wait_send()

            @pl.when(far)
            def _():
                hop_copy(f).wait_send()

            @pl.when(relays)
            def _():
                relay_copy(f).wait_send()
        else:
            @pl.when(has_low)
            def _():
                x_copy(0, f).wait_send()

            @pl.when(has_high)
            def _():
                x_copy(1, f).wait_send()

    barrier = pltpu.get_barrier_semaphore()
    for z in (left, right):
        pl.semaphore_signal(barrier, inc=1, device_id={"gz": z}, device_id_type=MESH)
    expected = 2
    for step in (-2, -1, 1, 2):
        there = (b + step >= 0) & (b + step < bricks)
        expected = expected + jnp.where(there, 1, 0)

        @pl.when(there)
        def _():
            pl.semaphore_signal(barrier, inc=1, device_id={"brick": b + step}, device_id_type=MESH)

    for copy in small + edges:
        copy.start()
    for f in range(fields):
        load(f).start()

    pl.semaphore_wait(barrier, expected)
    for f in range(early):
        send_lines(f, True)
    for way, there in enumerate((has_low, has_high)):
        @pl.when(there)
        def _():
            for copy in neighbour_copies(way):
                copy.start()

    rows = cells + 16
    i = lax.broadcasted_iota(jnp.int32, (rows, 2 * cells), 0)
    j = lax.rem(lax.broadcasted_iota(jnp.int32, (rows, 2 * cells), 1), cells)
    n = i - j
    main = i < cells
    to_right, to_left = i == cells, i == cells + 8
    dist = jnp.where(main, jnp.abs(n), jnp.where(to_right, cells - 1 - j, j))
    side = jnp.where(n > 0, 1.0, jnp.where(n < 0, -1.0, 0.0))
    tab[0] = dist.astype(f32)
    tab[1] = jnp.where(main, side, jnp.where(to_right | to_left, 1.0, 0.0)) * parity(dist)
    tab[2] = jnp.where(main & (dist == 1), side, 0.0)
    pick = ((i == cells + 1) & (j == cells - 1)) | ((i == cells + 9) & (j == 0))
    tab[3] = jnp.where(pick, 1.0, 0.0)
    ie = lax.broadcasted_iota(jnp.int32, (cells, LANES), 0)
    etab[0] = (ie + 1).astype(f32)
    etab[1] = parity(ie + 1)
    etab[2] = (cells - ie).astype(f32)
    etab[3] = -parity(cells - ie)

    @pl.when(jnp.logical_not(has_low))
    def _():
        gv[:, 0] = jnp.zeros((fields, cells, width), f32)

    @pl.when(jnp.logical_not(has_high))
    def _():
        gv[:, lines + 1] = jnp.zeros((fields, cells, width), f32)

    for copy in small:
        copy.wait()
    diagonal = lax.broadcasted_iota(jnp.int32, (lines, lines), 0) == lax.broadcasted_iota(
        jnp.int32, (lines, lines), 1
    )
    for k, values in enumerate(line_coefs(alpha_v[...])):
        for f in range(fields):
            column = jnp.sum(jnp.where(diagonal, values[f : f + 1], 0.0), axis=1, keepdims=True)
            coef[k, f, :lines] = jnp.broadcast_to(column, (lines, LANES))
    for k in range(2):
        metrics[k, :lines] = jnp.concatenate([metric_v[k], metric_v[k]], axis=1)

    def line_values(f, x):
        return (coef[k, f, pl.ds(x, 1), :] for k in range(3))

    def product(ps, f, x, values, keep=True):
        if ps == 0:
            log_ratio, amp, delta = line_values(f, x)
            powers = tab[1] * jnp.exp(tab[0] * log_ratio)
            mat = jnp.concatenate([powers[:cells] * amp, powers[cells:]], axis=0)
            mat = mat + tab[2] * delta + tab[3]
            if keep:
                mats[f, x] = mat
        else:
            mat = mats[f, x]
        mat = mat * metrics[ps, pl.ds(x, 1), :]
        high = mat.astype(bf16).astype(f32)
        column = lax.broadcasted_iota(jnp.int32, mat.shape, 1)
        split = jnp.where(column < cells, high, mat - high).astype(bf16)
        vh = values.astype(bf16)
        vl = (values - vh.astype(f32)).astype(bf16)
        return jnp.dot(
            jnp.concatenate([split, split], axis=1),
            jnp.concatenate([vh, vh, vl, vl], axis=0),
            preferred_element_type=f32,
        )

    def outgoing(ps, f, x, result):
        edge = isinstance(x, int)
        for kind in range(2):
            for way in range(2):
                at = cells + 8 * way + kind
                row = result[at : at + 1]
                if edge:
                    es[ps, f, int(x > 0), way, kind : kind + 1, :] = row
                else:
                    zs[ps, way, f, kind, pl.ds(x, 1), :] = row

    def inner(f, x):
        result = product(0, f, x, gv[f, x + 1])
        outgoing(0, f, x, result)
        gv[f, x + 1] = result[:cells]

    def outer(f, x):
        own = gv[f, x + 1]
        smooth = own - smooth_weight * (gv[f, x + 2] - 2.0 * own + gv[f, x])
        result = product(1, f, x, smooth)
        outgoing(1, f, x, result)
        o_ref[f, x] = result[:cells]

    def finish(ps, f, x, halo=None):
        ref, line = (gv, x + 1) if ps == 0 else (o_ref, x)
        if halo is not None:
            line = halo * (lines + 1)
        log_ratio, amp, delta = line_values(f, x)
        if ps == 0:
            from_left = amp * etab[1] * jnp.exp(etab[0] * log_ratio)
            from_right = amp * etab[3] * jnp.exp(etab[2] * log_ratio)
            if halo is None:
                weights[f, x, 0] = from_left
                weights[f, x, 1] = from_right
        else:
            from_left, from_right = weights[f, x, 0], weights[f, x, 1]
        ie8 = lax.broadcasted_iota(jnp.int32, (8, LANES), 0)
        first8 = jnp.where(ie8 == 0, delta, 0.0)
        last8 = jnp.where(ie8 == 7, -delta, 0.0)
        if isinstance(x, int):
            rows = er.at[ps, f, int(x > 0)] if halo is None else hx.at[f, halo]
            low, high, low1, high1 = (
                rows[way, kind : kind + 1, :] for kind in range(2) for way in range(2)
            )
        else:
            low, high, low1, high1 = (
                zr[ps, way, f, kind, pl.ds(x, 1), :] for kind in range(2) for way in range(2)
            )
        for c in range(0, width, LANES):
            cols = slice(c, c + LANES)
            value = ref[f, line, :, cols] + from_left * low[:, cols] + from_right * high[:, cols]
            head = value[:8] + first8 * low1[:, cols]
            tail = value[cells - 8 :] + last8 * high1[:, cols]
            ref[f, line, :, cols] = jnp.concatenate([head, value[8 : cells - 8], tail], axis=0)

    def loop(low, high, body, unroll=1):
        def step(x, _):
            body(x)
            return 0

        lax.fori_loop(low, high, step, 0, unroll=unroll)

    def both(copy, ps, f, act):
        for way in range(2):
            getattr(copy(ps, way, f), act)()

    for copy in edges:
        copy.wait()

    def edges_in(f):
        inner(f, 0)
        inner(f, last)
        both(e_copy, 0, f, "start")

    def inside_in(f):
        load(f).wait()
        loop(1, last, lambda x: inner(f, x), last - 1)
        both(z_copy, 0, f, "start")

    def edges_first(f):
        both(e_copy, 0, f, "wait_recv")
        finish(0, f, 0)
        finish(0, f, last)

        @pl.when(f >= early)
        def _():
            send_lines(f)

        @pl.when(f < early)
        def _():
            for way, there in enumerate((has_low, has_high)):
                @pl.when(there)
                def _():
                    row_copy(way, f).start()

    def inside_first(f):
        both(z_copy, 0, f, "wait_recv")
        loop(1, last, lambda x: finish(0, f, x), last - 1)

    def inside_out(f):
        loop(1, last, lambda x: outer(f, x), last - 1)
        both(z_copy, 1, f, "start")

    def inside_last(f):
        both(z_copy, 1, f, "wait_recv")
        loop(1, last, lambda x: finish(1, f, x), last - 1)

    loop(0, fields, edges_in)
    inside_in(0)
    loop(0, fields, edges_first)
    loop(0, early, relay)
    loop(1, fields, inside_in)
    loop(early, fields, relay)
    loop(0, fields, inside_first)
    loop(0, fields, inside_out)
    kept = min(2, fields)
    loop(0, fields - kept, inside_last)

    def halo_ready(side):
        for copy in neighbour_copies(1 - side):
            copy.wait_recv()
        line, row = (last, lines) if side == 0 else (0, lines + 1)
        for k, values in enumerate(line_coefs(alpha_n[side])):
            for f in range(early):
                coef[k, f, row : row + 1] = jnp.broadcast_to(values[f : f + 1, line : line + 1], (1, LANES))
        values = metric_n[side, line : line + 1, :]
        metrics[0, row : row + 1] = jnp.concatenate([values, values], axis=1)

    def halo_first(f, side):
        row_copy(1 - side, f).wait_recv()
        line = side * (lines + 1)
        gv[f, line] = product(0, f, lines + side, gv[f, line], False)[:cells]
        finish(0, f, lines + side, side)

    for side, there in enumerate((has_low, has_high)):
        @pl.when(there)
        def _():
            halo_ready(side)

    lag = 3

    def edges_last(t):
        @pl.when(t < fields)
        def _():
            wait_lines(t)

            @pl.when(t < early)
            def _():
                for side, there in enumerate((has_low, has_high)):
                    @pl.when(there)
                    def _():
                        halo_first(t, side)

            outer(t, 0)
            outer(t, last)
            both(e_copy, 1, t, "start")

        @pl.when((t >= fields) & (t < fields + kept))
        def _():
            inside_last(t - kept)

        @pl.when(t >= lag)
        def _():
            f = t - lag
            both(e_copy, 1, f, "wait_recv")
            finish(1, f, 0)
            finish(1, f, last)

    loop(0, fields + lag, edges_last)

    def drain(f):
        for ps in range(2):
            both(z_copy, ps, f, "wait_send")
            both(e_copy, ps, f, "wait_send")
        lines_sent(f)

    loop(0, fields, drain)
    for way, there in enumerate((has_low, has_high)):
        @pl.when(there)
        def _():
            for copy in neighbour_copies(way):
                copy.wait_send()
            for f in range(early):
                row_copy(way, f).wait_send()


def body(bricks, peers, grad_field, alpha_coef, metric_inner, metric_outer):
    fields, lines, cells, width = grad_field.shape
    dma = pltpu.SemaphoreType.DMA
    early = min(2, fields)
    far = pl.BlockSpec(memory_space=pltpu.HBM)
    return pl.pallas_call(
        functools.partial(kernel, bricks, peers, early),
        out_shape=jax.ShapeDtypeStruct(grad_field.shape, f32),
        in_specs=[far] * 4,
        out_specs=pl.BlockSpec(memory_space=pltpu.VMEM),
        scratch_shapes=[
            pltpu.VMEM((fields, lines + 2, cells, width), f32),
            pltpu.VMEM((fields, lines), f32),
            pltpu.VMEM((2, lines, cells), f32),
            pltpu.VMEM((2, fields, lines), f32),
            pltpu.VMEM((2, lines, cells), f32),
            pltpu.VMEM((2, lines + 8, 2 * cells), f32),
            pltpu.VMEM((3, fields, lines + 8, LANES), f32),
            pltpu.VMEM((fields, cells, width), f32),
            pltpu.VMEM((2, 2, fields, 2, lines, width), f32),
            pltpu.VMEM((2, 2, fields, 2, lines, width), f32),
            pltpu.VMEM((2, fields, 2, 2, 2, width), f32),
            pltpu.VMEM((2, fields, 2, 2, 2, width), f32),
            pltpu.VMEM((early, 2, 2, 2, width), f32),
            pltpu.VMEM((4, cells + 16, 2 * cells), f32),
            pltpu.VMEM((4, cells, LANES), f32),
            pltpu.VMEM((fields, lines, cells + 16, 2 * cells), f32),
            pltpu.VMEM((fields, lines, 2, cells, LANES), f32),
            dma((2, 2)), dma((2, 2)), dma((2, early)), dma((2, early)),
            dma((3,)), dma((2,)), dma((fields,)),
            dma((2, 2, fields)), dma((2, 2, fields)), dma((2, 2, fields)), dma((2, 2, fields)),
            dma((2, fields)), dma((2, fields)), dma((fields,)), dma((fields,)),
        ],
        compiler_params=pltpu.CompilerParams(
            collective_id=0, has_side_effects=True, vmem_limit_bytes=40 * 1024 * 1024
        ),
    )(*(pltpu.with_memory_space_constraint(a, pltpu.HBM) for a in (grad_field, alpha_coef, metric_inner, metric_outer)))


def solution(mesh):
    placed = (P(None, "brick", "gz", None), P(None, "brick"), P("brick", "gz"), P("brick", "gz"))
    return jax.shard_map(
        functools.partial(body, mesh.shape["brick"], mesh.shape["gz"]),
        mesh=mesh, in_specs=placed, out_specs=P(None, "brick", "gz", None), check_vma=False,
    )
```
